256 devices in a mesh: hid: 16 (over y, x_hi, core), wid: 16 (over z, x_lo).
Axes of the slice: x: 4 (x_hi: 2, x_lo: 2; x = x_hi * 2 + x_lo), y: 4, z: 8, core: 2. Of those that a mesh axis runs over, the one named last changes fastest.
Arguments:
- tokens: bfloat16 [512, 8192], P('hid', 'wid'), may hold values from -6 to 6
- gate_weight: bfloat16 [8192, 28672], P('wid', 'hid'), may hold values from -0.0625 to 0.0625
- up_weight: bfloat16 [8192, 28672], P('wid', 'hid'), may hold values from -0.0625 to 0.0625
- down_weight: bfloat16 [28672, 8192], P('hid', 'wid'), may hold values from -0.03125 to 0.03125
- cotangent: bfloat16 [512, 8192], P('hid', 'wid'), may hold values from -6 to 6
Outputs:
- output: bfloat16 [512, 8192], P('hid', 'wid')
- grad_tokens: bfloat16 [512, 8192], P('hid', 'wid')
- grad_gate: bfloat16 [8192, 28672], P('wid', 'hid')
- grad_up: bfloat16 [8192, 28672], P('wid', 'hid')
- grad_down: bfloat16 [28672, 8192], P('hid', 'wid')
The draws below stay inside these ranges and needn't reach their ends.
All inputs are finite; a program needn't handle non-finite values.
Results may differ from the reference program's by a relative error of at most 0.005.
Values may be sent and summed in bfloat16 or wider, within the bound.
No kernel may reach another device: no remote copies, remote signals or barrier semaphores. Data moves between devices by JAX's collectives and lax.ppermute only.
A program may use at most 128 MiB of HBM per device.

```python
import jax
import jax.numpy as jnp

D = 8192
FF = 28672
TOKENS = 512


def level_of(stream_key, extent, pieces, smallest, largest):
    level, own = 1.0, jax.random.fold_in(stream_key, 6)
    for axis_at, blocks in pieces:
        heights = jnp.exp(jax.random.uniform(jax.random.fold_in(own, axis_at), (blocks,), jnp.float32, smallest / len(pieces), largest / len(pieces)))
        level = level * jnp.repeat(heights, extent[axis_at] // blocks).reshape([-1 if axis == axis_at else 1 for axis in range(len(extent))])
    return level


def centred(rng, dims, spread, reach, shards=(), dtype=jnp.bfloat16):
    level = level_of(rng, dims, shards, -0.22, 0.18) if shards else 1.0
    result = jax.random.normal(rng, dims, jnp.float32) * spread * level
    return jnp.minimum(jnp.maximum(result, -reach), reach).astype(dtype)


def setup_inputs(seed: int = 0) -> dict:
    splits = jax.random.split(jax.random.key(seed), 6)
    tokens = centred(splits[0], (TOKENS, D), 1.0, 6.0, ((0, 16), (1, 16)))
    gate_weight = centred(splits[1], (D, FF), D ** -0.5, 0.0625, ((0, 16), (1, 16)))
    up_weight = centred(splits[2], (D, FF), D ** -0.5, 0.0625, ((0, 16), (1, 16)))
    down_weight = centred(splits[3], (FF, D), FF ** -0.5, 0.03125, ((0, 16), (1, 16)))
    cotangent = centred(splits[4], (TOKENS, D), 1.0, 6.0, ((0, 16), (1, 16)))
    return dict(tokens=tokens, gate_weight=gate_weight, up_weight=up_weight, down_weight=down_weight, cotangent=cotangent)


def reference(tokens, gate_weight, up_weight, down_weight, cotangent):
    gate = jnp.dot(tokens, gate_weight, preferred_element_type=jnp.float32)
    up = jnp.dot(tokens, up_weight, preferred_element_type=jnp.float32)
    dhidden = jnp.dot(cotangent, down_weight.T, preferred_element_type=jnp.float32)
    sig = jax.nn.sigmoid(gate)
    act = gate * sig
    hidden = (act * up).astype(jnp.bfloat16)
    output = jnp.dot(hidden, down_weight, preferred_element_type=jnp.float32).astype(jnp.bfloat16)
    dgate = (dhidden * up * sig * (1.0 + gate * (1.0 - sig))).astype(jnp.bfloat16)
    dup = (dhidden * act).astype(jnp.bfloat16)
    grad_tokens = (jnp.dot(dgate, gate_weight.T, preferred_element_type=jnp.float32)
                   + jnp.dot(dup, up_weight.T, preferred_element_type=jnp.float32)).astype(jnp.bfloat16)
    grad_gate = jnp.dot(tokens.T, dgate, preferred_element_type=jnp.float32).astype(jnp.bfloat16)
    grad_up = jnp.dot(tokens.T, dup, preferred_element_type=jnp.float32).astype(jnp.bfloat16)
    grad_down = jnp.dot(hidden.T, cotangent, preferred_element_type=jnp.float32).astype(jnp.bfloat16)
    return output, grad_tokens, grad_gate, grad_up, grad_down
```

```python
import functools

import jax
import jax.numpy as jnp
import numpy as np
from jax import lax
from jax.experimental import pallas as pl
from jax.experimental.pallas import tpu as pltpu
from jax.sharding import PartitionSpec as P

BF, F16, F32 = jnp.bfloat16, jnp.float16, jnp.float32
NY, NX, NZ = 4, 2, 8
SPLIT = 1024
MINE, BOTH = ((2, 4, 3), (6, 1, 7)), 5
VMEM = pl.BlockSpec(memory_space=pltpu.VMEM)
SMEM = pl.BlockSpec(memory_space=pltpu.SMEM)
LIMIT = pltpu.CompilerParams(vmem_limit_bytes=50 * 2**20)
SMALL = pltpu.CompilerParams(vmem_limit_bytes=12 * 2**20)
SCALE = 2.0**20


def hid_from(x, shift):
    pairs = []
    for y in range(NY):
        for h in range(NX):
            for c in range(2):
                dy, dx = divmod(shift[c], 2)
                pairs.append((((y + dy) % NY) * 4 + (h ^ dx) * 2 + c, y * 4 + h * 2 + c))
    return lax.ppermute(x, "hid", pairs)


def hid_to(x, shift):
    pairs = []
    for y in range(NY):
        for h in range(NX):
            for c in range(2):
                dy, dx = divmod(shift[c], 2)
                pairs.append((y * 4 + h * 2 + c, ((y + dy) % NY) * 4 + (h ^ dx) * 2 + c))
    return lax.ppermute(x, "hid", pairs)


def swap_core(x):
    return lax.ppermute(x, "hid", [(i, i ^ 1) for i in range(NY * NX * 2)])


def send_z(x, dz):
    pairs = [(z * 2 + l, ((z + dz) % NZ) * 2 + l) for z in range(NZ) for l in range(2)]
    return lax.ppermute(x, "wid", pairs)


def swap_x(x):
    return lax.ppermute(x, "wid", [(w, w ^ 1) for w in range(NZ * 2)])


def encode(v):
    root = jnp.sqrt(jnp.abs(v))
    return jnp.where(v < 0, -root, root).astype(F16)


def decode(w):
    w = w.astype(F32)
    return w * jnp.abs(w)


def together(*arrays):
    return lax.optimization_barrier(arrays)


def reduce_z(rings):
    made, state = [None] * len(rings), [None] * len(rings)
    turn = None
    for k in (4, 3, 2, 1):
        for n, (terms, far) in enumerate(rings):
            if k == 4:
                made[n] = terms(turn)
            term = made[n]
            out = [term(k * far)]
            if k > 1:
                out.append(term((1 - k) * far))
            if k < 4:
                out = [o + decode(s) for o, s in zip(out, state[n])]
            out = [encode(o) for o in out]
            if turn is not None:
                *out, _ = together(*out, turn)
            else:
                out = together(*out)
            turn = out[0]
            got = [send_z(o, d) for o, d in zip(out, (far, -far))]
            state[n] = got if k > 1 else got + state[n][1:]
    return [term(0) + decode(s[0]) + decode(s[1]) for term, s in zip(made, state)], (turn, state[-1][1])


class Gather:
    def __init__(self, own):
        self.up = self.down = own
        self.got = {0: own}

    def round(self, k, *after):
        up, down = self.up, self.down
        if k == 4:
            half = up.shape[1] // 2
            up, down = up[:, :half], down[:, half:]
        if k == 1:
            up, *_ = together(up, *after)
            down = up
        else:
            up, down, *_ = together(up, down, *after)
        self.up, self.down = send_z(up, 1), send_z(down, -1)
        if k < 4:
            self.got[8 - k], self.got[k] = self.up, self.down
        return up

    def blocks(self):
        return [*(self.got[k] for k in range(4)), self.up, self.down, *(self.got[k] for k in range(5, 8))]


def pointwise(gate, up, dhidden):
    sig = jax.nn.sigmoid(gate)
    act = gate * sig
    hidden = (act * up).astype(BF)
    dgate = (dhidden * up * sig * (1.0 + gate * (1.0 - sig))).astype(BF)
    dup = (dhidden * act).astype(BF)
    return jnp.stack([hidden, dgate, dup])


def place():
    wid, hid = lax.axis_index("wid"), lax.axis_index("hid")
    return wid // 2, wid % 2, hid % 2


def pick(c, n, own):
    a, b = MINE[0][n], MINE[1][n]
    return jnp.where((c == 0) == own, a, b)


def order_kernel(at, pair, mine, theirs, tok, ct, tok_rel, ct_rel, flat):
    z, l, c = at[0], at[1], at[2]
    nt = pair.shape[2]
    flat[0:2] = pair[...]
    flat[2:9] = mine[...]
    flat[9:16] = theirs[...]

    def source(q, d):
        s = jnp.where(q == 0, d, jnp.where(d == c, 8, 15))
        for core in range(2):
            for n in range(3):
                s = jnp.where(q == MINE[core][n], jnp.where(c == core, 2, 9) + 2 * n + d, s)
        return s

    for k in range(8):
        for i in range(2):
            block = flat[source(lax.rem(z + k, 8), lax.rem(l + i, 2))]
            for to, tc, row in ((tok, ct, 2 * k + i), (tok_rel, ct_rel, 8 * i + k)):
                rows = pl.ds(row * nt, nt)
                to[rows, :] = block[0]
                tc[rows, :] = block[1]


def order(at, pair, mine, theirs):
    nt, nd = pair.shape[2:]
    return pl.pallas_call(
        order_kernel,
        in_specs=[SMEM, VMEM, VMEM, VMEM],
        out_specs=[VMEM] * 4,
        out_shape=[jax.ShapeDtypeStruct((16 * nt, nd), BF)] * 4,
        scratch_shapes=[pltpu.VMEM((16, 2, nt, nd), BF)],
        compiler_params=SMALL,
        name="order",
    )(at, pair, mine, theirs)


def pair_kernel(at, own, other, pair):
    c = at[2]
    pair[c] = own[...]
    pair[1 - c] = other[...]


def pair_up(at, own, other):
    return pl.pallas_call(
        pair_kernel,
        in_specs=[SMEM, VMEM, VMEM],
        out_specs=VMEM,
        out_shape=jax.ShapeDtypeStruct((2, *own.shape), own.dtype),
        compiler_params=SMALL,
        name="pair",
    )(at, own, other)


def dot(a, b, ca, cb):
    return lax.dot_general(a, b, (((ca,), (cb,)), ((), ())), preferred_element_type=F32)


def block_of(cols):
    return 512 if cols == SPLIT else 256


def spec_of(a):
    lead = a.shape[:-1]
    return pl.BlockSpec((*lead, block_of(a.shape[-1])), lambda j: (0,) * len(lead) + (j,))


def load(refs, i):
    return jnp.concatenate([r[i] for r in refs], 0)


def add_products(j, acc, ins, dw, gw, uw):
    nd = dw.shape[1]

    @pl.when(j == 0)
    def _():
        acc[...] = jnp.zeros_like(acc)

    h, g, u = (load(ins, i) for i in range(3))
    last = (((1,), (1,)), ((), ()))
    acc[:, 0:nd] += jnp.dot(h, dw[...], preferred_element_type=F32)
    gt = lax.dot_general(g, gw[...], last, preferred_element_type=F32)
    acc[:, nd:] += gt + lax.dot_general(u, uw[...], last, preferred_element_type=F32)


def weight_specs(nd, first, cols):
    blk = block_of(cols)
    at = first // blk
    side = pl.BlockSpec((nd, blk), lambda j: (0, at + j))
    return [pl.BlockSpec((blk, nd), lambda j: (at + j, 0)), side, side]


def cost(rows, nd, cols):
    return pl.CostEstimate(flops=6 * rows * nd * cols, bytes_accessed=12 * nd * cols, transcendentals=0)


def part_kernel(*refs):
    ins, (dw, gw, uw, acc) = refs[:-4], refs[-4:]
    add_products(pl.program_id(0), acc, ins, dw, gw, uw)


def part_outputs(arrays, first, weights, nt):
    nd, cols = weights[0].shape[1], arrays[0].shape[-1]
    return pl.pallas_call(
        part_kernel,
        grid=(cols // block_of(cols),),
        in_specs=[spec_of(a) for a in arrays] + weight_specs(nd, first, cols),
        out_specs=pl.BlockSpec((16 * nt, 2 * nd), lambda j: (0, 0)),
        out_shape=jax.ShapeDtypeStruct((16 * nt, 2 * nd), F32),
        compiler_params=LIMIT,
        cost_estimate=cost(16 * nt, nd, cols),
        name="part_outputs",
    )(*arrays, *weights)


def out_kernel(steps, nt, at, fixed, *refs):
    j = pl.program_id(0)
    ins, (dw, gw, uw, give, keep, acc) = refs[:-6], refs[-6:]
    add_products(j, acc, ins, dw, gw, uw)

    @pl.when(j == steps - 1)
    def _():
        z, l, c = at[0], at[1], at[2]

        def block(q, d):
            rows = pl.ds(pl.multiple_of((2 * lax.rem(q + 8 - z, 8) + lax.rem(d + l, 2)) * nt, nt), nt)
            return fixed[rows, :] + acc[rows, :]

        for ref, own in ((give, False), (keep, True)):
            core = c if own else 1 - c
            for n in range(3):
                for d in range(2):
                    ref[2 * n + d] = block(pick(c, n, own), d).astype(ref.dtype)
            ref[6] = block(BOTH, core).astype(ref.dtype)
            ref[7] = block(0, core).astype(ref.dtype)


def outputs(at, fixed, arrays, first, weights, nt):
    nd, cols = weights[0].shape[1], arrays[0].shape[-1]
    whole = pl.BlockSpec((8, nt, 2 * nd), lambda j: (0, 0, 0))
    return pl.pallas_call(
        functools.partial(out_kernel, cols // block_of(cols), nt),
        grid=(cols // block_of(cols),),
        in_specs=[SMEM, VMEM] + [spec_of(a) for a in arrays] + weight_specs(nd, first, cols),
        out_specs=[whole, whole],
        out_shape=[jax.ShapeDtypeStruct((8, nt, 2 * nd), BF), jax.ShapeDtypeStruct((8, nt, 2 * nd), F32)],
        scratch_shapes=[pltpu.VMEM((16 * nt, 2 * nd), F32)],
        compiler_params=LIMIT,
        cost_estimate=cost(16 * nt, nd, cols),
        name="outputs",
    )(at, fixed, *arrays, *weights)


def grads_kernel(count, tok, ct, *refs):
    ins, (gg, gu, gd, tt) = refs[:count], refs[-4:]

    @pl.when(pl.program_id(0) == 0)
    def _():
        tt[...] = tok[...].T

    h, g, u = (load(ins, i) for i in range(3))
    gg[...] = jnp.dot(tt[...], g, preferred_element_type=F32).astype(BF)
    gu[...] = jnp.dot(tt[...], u, preferred_element_type=F32).astype(BF)
    gd[...] = jnp.dot(h.T, ct[...], preferred_element_type=F32).astype(BF)


def grads(arrays, first, tok, ct, nf, into=()):
    (rows, nd), cols = tok.shape, arrays[0].shape[-1]
    blk = block_of(cols)
    side = pl.BlockSpec((nd, blk), lambda j: (0, first // blk + j))
    wide, tall = jax.ShapeDtypeStruct((nd, nf), BF), jax.ShapeDtypeStruct((nf, nd), BF)
    before = 2 + len(arrays)
    return pl.pallas_call(
        functools.partial(grads_kernel, len(arrays)),
        grid=(cols // blk,),
        in_specs=[VMEM, VMEM] + [spec_of(a) for a in arrays] + [pl.BlockSpec(memory_space=pl.ANY)] * len(into),
        out_specs=[side, side, pl.BlockSpec((blk, nd), lambda j: (first // blk + j, 0))],
        out_shape=[wide, wide, tall],
        scratch_shapes=[pltpu.VMEM((nd, rows), BF)],
        input_output_aliases={before + i: i for i in range(len(into))},
        compiler_params=LIMIT,
        cost_estimate=cost(rows, nd, cols),
        name="grads",
    )(tok, ct, *arrays, *into)


def per_device(tokens, gate_weight, up_weight, down_weight, cotangent):
    nt, nd = tokens.shape
    nf = gate_weight.shape[1]
    z, l, c = place()
    at = jnp.stack([z, l, c])

    def by_core(a, b):
        return jnp.where(c == 0, a, b), jnp.where(c == 0, b, a)

    own = jnp.stack([tokens, cotangent])
    own, other = lax.optimization_barrier((own, swap_core(own)))
    pair = pair_up(at, own, other)
    got = [hid_from(pair, (a, b)) for a, b in zip(*MINE)]
    mine = jnp.concatenate(got + [hid_from(own, (BOTH, BOTH))[None]], 0)
    tok, ct, tok_rel, ct_rel = order(at, pair, mine, swap_core(mine))

    weights = down_weight, gate_weight, up_weight

    def terms(cols, after):
        t, g = tok_rel, ct_rel
        if after is not None:
            t, g, _ = together(t, g, after)
        out = [dot(t, gate_weight[:, cols], 1, 0), dot(t, up_weight[:, cols], 1, 0), dot(g, down_weight[cols], 1, 1)]
        out = [(p * SCALE).reshape(2, 8, nt, p.shape[1]) for p in out]
        return lambda k: jnp.stack([p[:, k % 8] for p in out])

    def finish(total, *after):
        mine, *_ = together(encode(total), *after)
        total = total + decode(swap_x(mine))[:, ::-1]
        return pointwise(*(total * (1.0 / SCALE))).reshape(3, 2 * nt, -1), mine

    xcols, zcols = slice(0, SPLIT), slice(SPLIT, None)
    (zsum, xsum), after = reduce_z([(functools.partial(terms, zcols), 1), (functools.partial(terms, xcols), -1)])
    zown, _ = finish(zsum)
    zring = Gather(zown)
    sent = zring.round(1, *after)
    xown, mine = finish(xsum, sent)
    sent = zring.round(2, mine)
    xring = Gather(xown)
    sent = xring.round(1, sent)
    sent = zring.round(3, sent)
    sent = xring.round(2, sent)
    sent = zring.round(4, sent)
    sent = xring.round(3, sent)
    zall = zring.blocks()
    fixed = part_outputs(zall, SPLIT, weights, nt)
    xring.round(4, fixed)
    xall = xring.blocks()
    part = grads(zall, SPLIT, tok, ct, nf)

    give, keep = outputs(at, fixed, xall, 0, weights, nt)

    keep = keep + swap_core(give).astype(F32)
    sent = keep.astype(BF)
    got = [hid_to(sent[2 * n : 2 * n + 2], (MINE[0][n], MINE[1][n])) for n in range(3)]
    got.append(hid_to(sent[6], (BOTH, BOTH)))
    got = together(*got, *grads(xall, 0, tok, ct, nf, part))
    grad_gate, grad_up, grad_down = got[4:]
    total = sum(g.astype(F32) for g in got[:3])
    total_own, total_other = by_core(total[0], total[1])
    total = total_own + got[3].astype(F32) + keep[7] + swap_core(total_other)
    output, grad_tokens = total[:, :nd].astype(BF), total[:, nd:].astype(BF)
    return (output, grad_tokens, grad_gate, grad_up, grad_down)


def solution(mesh):
    return jax.shard_map(
        per_device,
        mesh=mesh,
        in_specs=(
            P("hid", "wid"),
            P("wid", "hid"),
            P("wid", "hid"),
            P("hid", "wid"),
            P("hid", "wid"),
        ),
        out_specs=(
            P("hid", "wid"),
            P("hid", "wid"),
            P("wid", "hid"),
            P("wid", "hid"),
            P("hid", "wid"),
        ),
        check_vma=False,
    )
```

```python
import functools

import jax
import jax.numpy as jnp
import numpy as np
from jax import lax
from jax.experimental import pallas as pl
from jax.experimental.pallas import tpu as pltpu
from jax.sharding import PartitionSpec as P

BF, F16, F32 = jnp.bfloat16, jnp.float16, jnp.float32
NY, NX, NZ = 4, 2, 8
SPLIT = 1024
MINE, BOTH = ((2, 4, 3), (6, 1, 7)), 5
VMEM = pl.BlockSpec(memory_space=pltpu.VMEM)
SMEM = pl.BlockSpec(memory_space=pltpu.SMEM)
LIMIT = pltpu.CompilerParams(vmem_limit_bytes=50 * 2**20)
SMALL = pltpu.CompilerParams(vmem_limit_bytes=12 * 2**20)
SCALE = 2.0**20


def hid_from(x, shift):
    pairs = []
    for y in range(NY):
        for h in range(NX):
            for c in range(2):
                dy, dx = divmod(shift[c], 2)
                pairs.append((((y + dy) % NY) * 4 + (h ^ dx) * 2 + c, y * 4 + h * 2 + c))
    return lax.ppermute(x, "hid", pairs)


def hid_to(x, shift):
    pairs = []
    for y in range(NY):
        for h in range(NX):
            for c in range(2):
                dy, dx = divmod(shift[c], 2)
                pairs.append((y * 4 + h * 2 + c, ((y + dy) % NY) * 4 + (h ^ dx) * 2 + c))
    return lax.ppermute(x, "hid", pairs)


def swap_core(x):
    return lax.ppermute(x, "hid", [(i, i ^ 1) for i in range(NY * NX * 2)])


def send_z(x, dz):
    pairs = [(z * 2 + l, ((z + dz) % NZ) * 2 + l) for z in range(NZ) for l in range(2)]
    return lax.ppermute(x, "wid", pairs)


def swap_x(x):
    return lax.ppermute(x, "wid", [(w, w ^ 1) for w in range(NZ * 2)])


def encode(v):
    root = jnp.sqrt(jnp.abs(v))
    return jnp.where(v < 0, -root, root).astype(F16)


def decode(w):
    w = w.astype(F32)
    return w * jnp.abs(w)


def together(*arrays):
    return lax.optimization_barrier(arrays)


def reduce_z(rings):
    made, state = [None] * len(rings), [None] * len(rings)
    turn = None
    for k in (4, 3, 2, 1):
        for n, (terms, far) in enumerate(rings):
            if k == 4:
                made[n] = terms(turn)
            term = made[n]
            out = [term(k * far)]
            if k > 1:
                out.append(term((1 - k) * far))
            if k < 4:
                out = [o + decode(s) for o, s in zip(out, state[n])]
            out = [encode(o) for o in out]
            if turn is not None:
                *out, _ = together(*out, turn)
            else:
                out = together(*out)
            turn = out[0]
            got = [send_z(o, d) for o, d in zip(out, (far, -far))]
            state[n] = got if k > 1 else got + state[n][1:]
    return [term(0) + decode(s[0]) + decode(s[1]) for term, s in zip(made, state)], (turn, state[-1][1])


class Gather:
    def __init__(self, own):
        self.up = self.down = own
        self.got = {0: own}

    def round(self, k, *after):
        up, down = self.up, self.down
        if k == 4:
            half = up.shape[1] // 2
            up, down = up[:, :half], down[:, half:]
        if k == 1:
            up, *_ = together(up, *after)
            down = up
        else:
            up, down, *_ = together(up, down, *after)
        self.up, self.down = send_z(up, 1), send_z(down, -1)
        if k < 4:
            self.got[8 - k], self.got[k] = self.up, self.down
        return up

    def blocks(self):
        return [*(self.got[k] for k in range(4)), self.up, self.down, *(self.got[k] for k in range(5, 8))]


def pointwise(gate, up, dhidden):
    sig = jax.nn.sigmoid(gate)
    act = gate * sig
    hidden = (act * up).astype(BF)
    dgate = (dhidden * up * sig * (1.0 + gate * (1.0 - sig))).astype(BF)
    dup = (dhidden * act).astype(BF)
    return jnp.stack([hidden, dgate, dup])


def place():
    wid, hid = lax.axis_index("wid"), lax.axis_index("hid")
    return wid // 2, wid % 2, hid % 2


def pick(c, n, own):
    a, b = MINE[0][n], MINE[1][n]
    return jnp.where((c == 0) == own, a, b)


def order_kernel(at, pair, mine, theirs, tok, ct, tok_rel, ct_rel, flat):
    z, l, c = at[0], at[1], at[2]
    nt = pair.shape[2]
    flat[0:2] = pair[...]
    flat[2:9] = mine[...]
    flat[9:16] = theirs[...]

    def source(q, d):
        s = jnp.where(q == 0, d, jnp.where(d == c, 8, 15))
        for core in range(2):
            for n in range(3):
                s = jnp.where(q == MINE[core][n], jnp.where(c == core, 2, 9) + 2 * n + d, s)
        return s

    for k in range(8):
        for i in range(2):
            block = flat[source(lax.rem(z + k, 8), lax.rem(l + i, 2))]
            for to, tc, row in ((tok, ct, 2 * k + i), (tok_rel, ct_rel, 8 * i + k)):
                rows = pl.ds(row * nt, nt)
                to[rows, :] = block[0]
                tc[rows, :] = block[1]


def order(at, pair, mine, theirs):
    nt, nd = pair.shape[2:]
    return pl.pallas_call(
        order_kernel,
        in_specs=[SMEM, VMEM, VMEM, VMEM],
        out_specs=[VMEM] * 4,
        out_shape=[jax.ShapeDtypeStruct((16 * nt, nd), BF)] * 4,
        scratch_shapes=[pltpu.VMEM((16, 2, nt, nd), BF)],
        compiler_params=SMALL,
        name="order",
    )(at, pair, mine, theirs)


def pair_kernel(at, own, other, pair):
    c = at[2]
    pair[c] = own[...]
    pair[1 - c] = other[...]


def pair_up(at, own, other):
    return pl.pallas_call(
        pair_kernel,
        in_specs=[SMEM, VMEM, VMEM],
        out_specs=VMEM,
        out_shape=jax.ShapeDtypeStruct((2, *own.shape), own.dtype),
        compiler_params=SMALL,
        name="pair",
    )(at, own, other)


def dot(a, b, ca, cb):
    return lax.dot_general(a, b, (((ca,), (cb,)), ((), ())), preferred_element_type=F32)


def block_of(cols):
    return 512 if cols == SPLIT else 256


def spec_of(a):
    lead = a.shape[:-1]
    return pl.BlockSpec((*lead, block_of(a.shape[-1])), lambda j: (0,) * len(lead) + (j,))


def load(refs, i):
    return jnp.concatenate([r[i] for r in refs], 0)


def add_products(j, acc, ins, dw, gw, uw):
    nd = dw.shape[1]

    @pl.when(j == 0)
    def _():
        acc[...] = jnp.zeros_like(acc)

    h, g, u = (load(ins, i) for i in range(3))
    last = (((1,), (1,)), ((), ()))
    acc[:, 0:nd] += jnp.dot(h, dw[...], preferred_element_type=F32)
    gt = lax.dot_general(g, gw[...], last, preferred_element_type=F32)
    acc[:, nd:] += gt + lax.dot_general(u, uw[...], last, preferred_element_type=F32)


def add_grads(tok, ct, ins, gg, gu, gd, tt):
    @pl.when(pl.program_id(0) == 0)
    def _():
        tt[...] = tok[...].T

    h, g, u = (load(ins, i) for i in range(3))
    gg[...] = jnp.dot(tt[...], g, preferred_element_type=F32).astype(BF)
    gu[...] = jnp.dot(tt[...], u, preferred_element_type=F32).astype(BF)
    gd[...] = jnp.dot(h.T, ct[...], preferred_element_type=F32).astype(BF)


def grad_outs(nd, nf, first, cols):
    blk = block_of(cols)
    side = pl.BlockSpec((nd, blk), lambda j: (0, first // blk + j))
    wide, tall = jax.ShapeDtypeStruct((nd, nf), BF), jax.ShapeDtypeStruct((nf, nd), BF)
    return [side, side, pl.BlockSpec((blk, nd), lambda j: (first // blk + j, 0))], [wide, wide, tall]


def weight_specs(nd, first, cols):
    blk = block_of(cols)
    at = first // blk
    side = pl.BlockSpec((nd, blk), lambda j: (0, at + j))
    return [pl.BlockSpec((blk, nd), lambda j: (at + j, 0)), side, side]


def cost(rows, nd, cols):
    return pl.CostEstimate(flops=6 * rows * nd * cols, bytes_accessed=12 * nd * cols, transcendentals=0)


def part_kernel(tok, ct, *refs):
    ins, (dw, gw, uw, acc, gg, gu, gd, tt) = refs[:-8], refs[-8:]
    add_products(pl.program_id(0), acc, ins, dw, gw, uw)
    add_grads(tok, ct, ins, gg, gu, gd, tt)


def part(tok, ct, arrays, first, weights):
    (rows, nd), cols = tok.shape, arrays[0].shape[-1]
    specs, shapes = grad_outs(nd, weights[0].shape[0], first, cols)
    return pl.pallas_call(
        part_kernel,
        grid=(cols // block_of(cols),),
        in_specs=[VMEM, VMEM] + [spec_of(a) for a in arrays] + weight_specs(nd, first, cols),
        out_specs=[pl.BlockSpec((rows, 2 * nd), lambda j: (0, 0)), *specs],
        out_shape=[jax.ShapeDtypeStruct((rows, 2 * nd), F32), *shapes],
        scratch_shapes=[pltpu.VMEM((nd, rows), BF)],
        compiler_params=LIMIT,
        cost_estimate=cost(rows, nd, 2 * cols),
        name="part",
    )(tok, ct, *arrays, *weights)


def out_kernel(steps, nt, at, fixed, *refs):
    j = pl.program_id(0)
    ins, (dw, gw, uw, give, keep, acc) = refs[:-6], refs[-6:]
    add_products(j, acc, ins, dw, gw, uw)

    @pl.when(j == steps - 1)
    def _():
        z, l, c = at[0], at[1], at[2]

        def block(q, d):
            rows = pl.ds(pl.multiple_of((2 * lax.rem(q + 8 - z, 8) + lax.rem(d + l, 2)) * nt, nt), nt)
            return fixed[rows, :] + acc[rows, :]

        for ref, own in ((give, False), (keep, True)):
            core = c if own else 1 - c
            for n in range(3):
                for d in range(2):
                    ref[2 * n + d] = block(pick(c, n, own), d).astype(ref.dtype)
            ref[6] = block(BOTH, core).astype(ref.dtype)
            ref[7] = block(0, core).astype(ref.dtype)


def outputs(at, fixed, arrays, first, weights, nt):
    nd, cols = weights[0].shape[1], arrays[0].shape[-1]
    whole = pl.BlockSpec((8, nt, 2 * nd), lambda j: (0, 0, 0))
    return pl.pallas_call(
        functools.partial(out_kernel, cols // block_of(cols), nt),
        grid=(cols // block_of(cols),),
        in_specs=[SMEM, VMEM] + [spec_of(a) for a in arrays] + weight_specs(nd, first, cols),
        out_specs=[whole, whole],
        out_shape=[jax.ShapeDtypeStruct((8, nt, 2 * nd), BF), jax.ShapeDtypeStruct((8, nt, 2 * nd), F32)],
        scratch_shapes=[pltpu.VMEM((16 * nt, 2 * nd), F32)],
        compiler_params=LIMIT,
        cost_estimate=cost(16 * nt, nd, cols),
        name="outputs",
    )(at, fixed, *arrays, *weights)


def grads_kernel(count, tok, ct, *refs):
    add_grads(tok, ct, refs[:count], *refs[-4:])


def grads(arrays, first, tok, ct, nf, into):
    (rows, nd), cols = tok.shape, arrays[0].shape[-1]
    specs, shapes = grad_outs(nd, nf, first, cols)
    before = 2 + len(arrays)
    return pl.pallas_call(
        functools.partial(grads_kernel, len(arrays)),
        grid=(cols // block_of(cols),),
        in_specs=[VMEM, VMEM] + [spec_of(a) for a in arrays] + [pl.BlockSpec(memory_space=pl.ANY)] * len(into),
        out_specs=specs,
        out_shape=shapes,
        scratch_shapes=[pltpu.VMEM((nd, rows), BF)],
        input_output_aliases={before + i: i for i in range(len(into))},
        compiler_params=LIMIT,
        cost_estimate=cost(rows, nd, cols),
        name="grads",
    )(tok, ct, *arrays, *into)


def per_device(tokens, gate_weight, up_weight, down_weight, cotangent):
    nt, nd = tokens.shape
    nf = gate_weight.shape[1]
    z, l, c = place()
    at = jnp.stack([z, l, c])

    def by_core(a, b):
        return jnp.where(c == 0, a, b), jnp.where(c == 0, b, a)

    own = jnp.stack([tokens, cotangent])
    own, other = lax.optimization_barrier((own, swap_core(own)))
    pair = pair_up(at, own, other)
    got = [hid_from(pair, (a, b)) for a, b in zip(*MINE)]
    mine = jnp.concatenate(got + [hid_from(own, (BOTH, BOTH))[None]], 0)
    xcols, zcols = slice(0, SPLIT), slice(SPLIT, None)
    sides = [(gate_weight[:, c], up_weight[:, c], down_weight[c]) for c in (zcols, xcols)]
    mine, *sides = together(mine, *sides)
    tok, ct, tok_rel, ct_rel = order(at, pair, mine, swap_core(mine))

    weights = down_weight, gate_weight, up_weight

    def terms(gate, up, down, after):
        t, g = tok_rel, ct_rel
        if after is not None:
            t, g, _ = together(t, g, after)
        out = [dot(t, gate, 1, 0), dot(t, up, 1, 0), dot(g, down, 1, 1)]
        out = [(p * SCALE).reshape(2, 8, nt, p.shape[1]) for p in out]
        return lambda k: jnp.stack([p[:, k % 8] for p in out])

    def finish(total, *after):
        mine, *_ = together(encode(total), *after)
        total = total + decode(swap_x(mine))[:, ::-1]
        return pointwise(*(total * (1.0 / SCALE))).reshape(3, 2 * nt, -1), mine

    (zsum, xsum), after = reduce_z([(functools.partial(terms, *w), far) for w, far in zip(sides, (1, -1))])
    zown, _ = finish(zsum)
    zring = Gather(zown)
    sent = zring.round(1, *after)
    xown, mine = finish(xsum, sent)
    sent = zring.round(2, mine)
    xring = Gather(xown)
    sent = xring.round(1, sent)
    sent = zring.round(3, sent)
    sent = xring.round(2, sent)
    sent = zring.round(4, sent)
    sent = xring.round(3, sent)
    sent = xring.round(4, sent)
    *zall, _ = together(*zring.blocks(), sent)
    fixed, *begun = part(tok, ct, zall, SPLIT, weights)
    fixed, *xall = together(fixed, *xring.blocks())

    give, keep = outputs(at, fixed, xall, 0, weights, nt)

    keep = keep + swap_core(give).astype(F32)
    sent = keep.astype(BF)
    got = [hid_to(sent[2 * n : 2 * n + 2], (MINE[0][n], MINE[1][n])) for n in range(3)]
    got.append(hid_to(sent[6], (BOTH, BOTH)))
    got = together(*got, *grads(xall, 0, tok, ct, nf, begun))
    grad_gate, grad_up, grad_down = got[4:]
    total = sum(g.astype(F32) for g in got[:3])
    total_own, total_other = by_core(total[0], total[1])
    total = total_own + got[3].astype(F32) + keep[7] + swap_core(total_other)
    output, grad_tokens = total[:, :nd].astype(BF), total[:, nd:].astype(BF)
    return (output, grad_tokens, grad_gate, grad_up, grad_down)


def solution(mesh):
    return jax.shard_map(
        per_device,
        mesh=mesh,
        in_specs=(
            P("hid", "wid"),
            P("wid", "hid"),
            P("wid", "hid"),
            P("hid", "wid"),
            P("hid", "wid"),
        ),
        out_specs=(
            P("hid", "wid"),
            P("hid", "wid"),
            P("wid", "hid"),
            P("wid", "hid"),
            P("hid", "wid"),
        ),
        check_vma=False,
    )
```

```python
import functools

import jax
import jax.numpy as jnp
import numpy as np
from jax import lax
from jax.experimental import pallas as pl
from jax.experimental.pallas import tpu as pltpu
from jax.sharding import PartitionSpec as P

BF, F16, F32 = jnp.bfloat16, jnp.float16, jnp.float32
NY, NX, NZ = 4, 2, 8
SPLIT = 1024
MINE, BOTH = ((2, 4, 3), (6, 1, 7)), 5
VMEM = pl.BlockSpec(memory_space=pltpu.VMEM)
SMEM = pl.BlockSpec(memory_space=pltpu.SMEM)
LIMIT = pltpu.CompilerParams(vmem_limit_bytes=50 * 2**20)
SMALL = pltpu.CompilerParams(vmem_limit_bytes=12 * 2**20)
SCALE = 2.0**20


def hid_from(x, shift):
    pairs = []
    for y in range(NY):
        for h in range(NX):
            for c in range(2):
                dy, dx = divmod(shift[c], 2)
                pairs.append((((y + dy) % NY) * 4 + (h ^ dx) * 2 + c, y * 4 + h * 2 + c))
    return lax.ppermute(x, "hid", pairs)


def hid_to(x, shift):
    pairs = []
    for y in range(NY):
        for h in range(NX):
            for c in range(2):
                dy, dx = divmod(shift[c], 2)
                pairs.append((y * 4 + h * 2 + c, ((y + dy) % NY) * 4 + (h ^ dx) * 2 + c))
    return lax.ppermute(x, "hid", pairs)


def swap_core(x):
    return lax.ppermute(x, "hid", [(i, i ^ 1) for i in range(NY * NX * 2)])


def send_z(x, dz):
    pairs = [(z * 2 + l, ((z + dz) % NZ) * 2 + l) for z in range(NZ) for l in range(2)]
    return lax.ppermute(x, "wid", pairs)


def swap_x(x):
    return lax.ppermute(x, "wid", [(w, w ^ 1) for w in range(NZ * 2)])


def encode(v):
    root = jnp.sqrt(jnp.abs(v))
    return jnp.where(v < 0, -root, root).astype(F16)


def decode(w):
    w = w.astype(F32)
    return w * jnp.abs(w)


def together(*arrays):
    return lax.optimization_barrier(arrays)


def reduce_z(rings):
    made, state = [None] * len(rings), [None] * len(rings)
    turn = None
    for k in (4, 3, 2, 1):
        for n, (terms, far) in enumerate(rings):
            if k == 4:
                made[n] = terms(turn)
            term = made[n]
            out = [term(k * far)]
            if k > 1:
                out.append(term((1 - k) * far))
            if k < 4:
                out = [o + decode(s) for o, s in zip(out, state[n])]
            out = [encode(o) for o in out]
            if turn is not None:
                *out, _ = together(*out, turn)
            else:
                out = together(*out)
            turn = out[0]
            got = [send_z(o, d) for o, d in zip(out, (far, -far))]
            state[n] = got if k > 1 else got + state[n][1:]
    return [term(0) + decode(s[0]) + decode(s[1]) for term, s in zip(made, state)], (turn, state[-1][1])


class Gather:
    def __init__(self, own):
        self.up = self.down = own
        self.got = {0: own}

    def round(self, k, *after):
        up, down = self.up, self.down
        if k == 4:
            half = up.shape[1] // 2
            up, down = up[:, :half], down[:, half:]
        if k == 1:
            up, *_ = together(up, *after)
            down = up
        else:
            up, down, *_ = together(up, down, *after)
        self.up, self.down = send_z(up, 1), send_z(down, -1)
        if k < 4:
            self.got[8 - k], self.got[k] = self.up, self.down
        return up

    def blocks(self):
        return [*(self.got[k] for k in range(4)), self.up, self.down, *(self.got[k] for k in range(5, 8))]


def pointwise(gate, up, dhidden):
    sig = jax.nn.sigmoid(gate)
    act = gate * sig
    hidden = (act * up).astype(BF)
    dgate = (dhidden * up * sig * (1.0 + gate * (1.0 - sig))).astype(BF)
    dup = (dhidden * act).astype(BF)
    return jnp.stack([hidden, dgate, dup])


def place():
    wid, hid = lax.axis_index("wid"), lax.axis_index("hid")
    return wid // 2, wid % 2, hid % 2


def pick(c, n, own):
    a, b = MINE[0][n], MINE[1][n]
    return jnp.where((c == 0) == own, a, b)


def order_kernel(at, pair, mine, theirs, tok, ct, tok_rel, ct_rel, flat):
    z, l, c = at[0], at[1], at[2]
    nt = pair.shape[2]
    flat[0:2] = pair[...]
    flat[2:9] = mine[...]
    flat[9:16] = theirs[...]

    def source(q, d):
        s = jnp.where(q == 0, d, jnp.where(d == c, 8, 15))
        for core in range(2):
            for n in range(3):
                s = jnp.where(q == MINE[core][n], jnp.where(c == core, 2, 9) + 2 * n + d, s)
        return s

    for k in range(8):
        for i in range(2):
            block = flat[source(lax.rem(z + k, 8), lax.rem(l + i, 2))]
            for to, tc, row in ((tok, ct, 2 * k + i), (tok_rel, ct_rel, 8 * i + k)):
                rows = pl.ds(row * nt, nt)
                to[rows, :] = block[0]
                tc[rows, :] = block[1]


def order(at, pair, mine, theirs):
    nt, nd = pair.shape[2:]
    return pl.pallas_call(
        order_kernel,
        in_specs=[SMEM, VMEM, VMEM, VMEM],
        out_specs=[VMEM] * 4,
        out_shape=[jax.ShapeDtypeStruct((16 * nt, nd), BF)] * 4,
        scratch_shapes=[pltpu.VMEM((16, 2, nt, nd), BF)],
        compiler_params=SMALL,
        name="order",
    )(at, pair, mine, theirs)


def pair_kernel(at, own, other, pair):
    c = at[2]
    pair[c] = own[...]
    pair[1 - c] = other[...]


def pair_up(at, own, other):
    return pl.pallas_call(
        pair_kernel,
        in_specs=[SMEM, VMEM, VMEM],
        out_specs=VMEM,
        out_shape=jax.ShapeDtypeStruct((2, *own.shape), own.dtype),
        compiler_params=SMALL,
        name="pair",
    )(at, own, other)


def dot(a, b, ca, cb):
    return lax.dot_general(a, b, (((ca,), (cb,)), ((), ())), preferred_element_type=F32)


def products_kernel(first, cols, t, g, dw, gw, uw, p, gv, uv, dv, sems):
    cut = pl.ds(first, cols)
    copies = [
        pltpu.make_async_copy(w, v, sems.at[i])
        for i, (w, v) in enumerate(((gw.at[:, cut], gv), (uw.at[:, cut], uv), (dw.at[cut], dv)))
    ]
    for copy in copies:
        copy.start()
    for i, copy in enumerate(copies):
        copy.wait()
        if i < 2:
            b = jnp.dot(t[...], (gv, uv)[i][...], preferred_element_type=F32)
        else:
            b = lax.dot_general(g[...], dv[...], (((1,), (1,)), ((), ())), preferred_element_type=F32)
        p[i] = (b * SCALE).reshape(p.shape[1:])


def products(t, g, first, cols, weights, nt):
    nd = t.shape[1]
    return pl.pallas_call(
        functools.partial(products_kernel, first, cols),
        in_specs=[VMEM, VMEM] + [pl.BlockSpec(memory_space=pltpu.HBM)] * 3,
        out_specs=VMEM,
        out_shape=jax.ShapeDtypeStruct((3, 2, 8, nt, cols), F32),
        scratch_shapes=[pltpu.VMEM((nd, cols), BF)] * 2 + [pltpu.VMEM((cols, nd), BF), pltpu.SemaphoreType.DMA((3,))],
        compiler_params=SMALL,
        cost_estimate=cost(16 * nt, nd, cols),
        name="products",
    )(t, g, *weights)


def spec_of(a):
    return pl.BlockSpec(a.shape, lambda j: (0,) * len(a.shape))


def side_of(nd, first, cols):
    return pl.BlockSpec((pl.Element(nd), pl.Element(cols)), lambda j: (0, first))


def end_of(nd, first, cols):
    return pl.BlockSpec((pl.Element(cols), pl.Element(nd)), lambda j: (first, 0))


def load(refs, i):
    return jnp.concatenate([r[i] for r in refs], 0)


def add_products(j, acc, ins, dw, gw, uw):
    nd = dw.shape[1]

    @pl.when(j == 0)
    def _():
        acc[...] = jnp.zeros_like(acc)

    h, g, u = (load(ins, i) for i in range(3))
    last = (((1,), (1,)), ((), ()))
    acc[:, 0:nd] += jnp.dot(h, dw[...], preferred_element_type=F32)
    gt = lax.dot_general(g, gw[...], last, preferred_element_type=F32)
    acc[:, nd:] += gt + lax.dot_general(u, uw[...], last, preferred_element_type=F32)


def add_grads(tok, ct, ins, gg, gu, gd, tt):
    @pl.when(pl.program_id(0) == 0)
    def _():
        tt[...] = tok[...].T

    h, g, u = (load(ins, i) for i in range(3))
    gg[...] = jnp.dot(tt[...], g, preferred_element_type=F32).astype(BF)
    gu[...] = jnp.dot(tt[...], u, preferred_element_type=F32).astype(BF)
    gd[...] = jnp.dot(h.T, ct[...], preferred_element_type=F32).astype(BF)


def grad_outs(nd, nf, first, cols):
    side = side_of(nd, first, cols)
    wide, tall = jax.ShapeDtypeStruct((nd, nf), BF), jax.ShapeDtypeStruct((nf, nd), BF)
    return [side, side, end_of(nd, first, cols)], [wide, wide, tall]


def weight_specs(nd, first, cols):
    side = side_of(nd, first, cols)
    return [end_of(nd, first, cols), side, side]


def cost(rows, nd, cols):
    return pl.CostEstimate(flops=6 * rows * nd * cols, bytes_accessed=12 * nd * cols, transcendentals=0)


def part_kernel(tok, ct, *refs):
    ins, (dw, gw, uw, acc, gg, gu, gd, tt) = refs[:-8], refs[-8:]
    add_products(pl.program_id(0), acc, ins, dw, gw, uw)
    add_grads(tok, ct, ins, gg, gu, gd, tt)


def part(tok, ct, arrays, first, weights):
    (rows, nd), cols = tok.shape, arrays[0].shape[-1]
    specs, shapes = grad_outs(nd, weights[0].shape[0], first, cols)
    return pl.pallas_call(
        part_kernel,
        grid=(1,),
        in_specs=[VMEM, VMEM] + [spec_of(a) for a in arrays] + weight_specs(nd, first, cols),
        out_specs=[pl.BlockSpec((rows, 2 * nd), lambda j: (0, 0)), *specs],
        out_shape=[jax.ShapeDtypeStruct((rows, 2 * nd), F32), *shapes],
        scratch_shapes=[pltpu.VMEM((nd, rows), BF)],
        compiler_params=LIMIT,
        cost_estimate=cost(rows, nd, 2 * cols),
        name="part",
    )(tok, ct, *arrays, *weights)


def out_kernel(steps, nt, at, fixed, *refs):
    j = pl.program_id(0)
    ins, (dw, gw, uw, give, keep, acc) = refs[:-6], refs[-6:]
    add_products(j, acc, ins, dw, gw, uw)

    @pl.when(j == steps - 1)
    def _():
        z, l, c = at[0], at[1], at[2]

        def block(q, d):
            rows = pl.ds(pl.multiple_of((2 * lax.rem(q + 8 - z, 8) + lax.rem(d + l, 2)) * nt, nt), nt)
            return fixed[rows, :] + acc[rows, :]

        for ref, own in ((give, False), (keep, True)):
            core = c if own else 1 - c
            for n in range(3):
                for d in range(2):
                    ref[2 * n + d] = block(pick(c, n, own), d).astype(ref.dtype)
            ref[6] = block(BOTH, core).astype(ref.dtype)
            ref[7] = block(0, core).astype(ref.dtype)


def outputs(at, fixed, arrays, first, weights, nt):
    nd, cols = weights[0].shape[1], arrays[0].shape[-1]
    whole = pl.BlockSpec((8, nt, 2 * nd), lambda j: (0, 0, 0))
    return pl.pallas_call(
        functools.partial(out_kernel, 1, nt),
        grid=(1,),
        in_specs=[SMEM, VMEM] + [spec_of(a) for a in arrays] + weight_specs(nd, first, cols),
        out_specs=[whole, whole],
        out_shape=[jax.ShapeDtypeStruct((8, nt, 2 * nd), BF), jax.ShapeDtypeStruct((8, nt, 2 * nd), F32)],
        scratch_shapes=[pltpu.VMEM((16 * nt, 2 * nd), F32)],
        compiler_params=LIMIT,
        cost_estimate=cost(16 * nt, nd, cols),
        name="outputs",
    )(at, fixed, *arrays, *weights)


def grads_kernel(count, tok, ct, *refs):
    add_grads(tok, ct, refs[:count], *refs[-4:])


def grads(arrays, first, tok, ct, nf, into):
    (rows, nd), cols = tok.shape, arrays[0].shape[-1]
    specs, shapes = grad_outs(nd, nf, first, cols)
    before = 2 + len(arrays)
    return pl.pallas_call(
        functools.partial(grads_kernel, len(arrays)),
        grid=(1,),
        in_specs=[VMEM, VMEM] + [spec_of(a) for a in arrays] + [pl.BlockSpec(memory_space=pl.ANY)] * len(into),
        out_specs=specs,
        out_shape=shapes,
        scratch_shapes=[pltpu.VMEM((nd, rows), BF)],
        input_output_aliases={before + i: i for i in range(len(into))},
        compiler_params=LIMIT,
        cost_estimate=cost(rows, nd, cols),
        name="grads",
    )(tok, ct, *arrays, *into)


def per_device(tokens, gate_weight, up_weight, down_weight, cotangent):
    nt, nd = tokens.shape
    nf = gate_weight.shape[1]
    z, l, c = place()
    at = jnp.stack([z, l, c])

    def by_core(a, b):
        return jnp.where(c == 0, a, b), jnp.where(c == 0, b, a)

    own = jnp.stack([tokens, cotangent])
    far = hid_from(own, (BOTH, BOTH))
    pair = pair_up(at, own, swap_core(own))
    got = [hid_from(pair, (a, b)) for a, b in zip(*MINE)]
    mine = jnp.concatenate(got + [far[None]], 0)
    zw = gate_weight[:, SPLIT:], up_weight[:, SPLIT:], down_weight[SPLIT:]
    mine, zw = together(mine, zw)
    tok, ct, tok_rel, ct_rel = order(at, pair, mine, swap_core(mine))

    weights = down_weight, gate_weight, up_weight

    def zterms(_):
        out = [dot(tok_rel, zw[0], 1, 0), dot(tok_rel, zw[1], 1, 0), dot(ct_rel, zw[2], 1, 1)]
        out = [(p * SCALE).reshape(2, 8, nt, nf - SPLIT) for p in out]
        return lambda k: jnp.stack([p[:, k % 8] for p in out])

    def xterms(after):
        t, g, _ = together(tok_rel, ct_rel, after)
        p = products(t, g, 0, SPLIT, weights, nt)
        return lambda k: p[:, :, k % 8]

    def finish(total, *after):
        mine, *_ = together(encode(total), *after)
        total = total + decode(swap_x(mine))[:, ::-1]
        return pointwise(*(total * (1.0 / SCALE))).reshape(3, 2 * nt, -1), mine

    (zsum, xsum), after = reduce_z([(zterms, 1), (xterms, -1)])
    zown, _ = finish(zsum)
    zring = Gather(zown)
    sent = zring.round(1, *after)
    xown, mine = finish(xsum, sent)
    sent = zring.round(2, mine)
    xring = Gather(xown)
    sent = xring.round(1, sent)
    sent = zring.round(3, sent)
    sent = xring.round(2, sent)
    sent = zring.round(4, sent)
    sent = xring.round(3, sent)
    sent = xring.round(4, sent)
    *zall, _ = together(*zring.blocks(), sent)
    fixed, *begun = part(tok, ct, zall, SPLIT, weights)
    fixed, *xall = together(fixed, *xring.blocks())

    give, keep = outputs(at, fixed, xall, 0, weights, nt)

    keep = keep + swap_core(give).astype(F32)
    sent = keep.astype(BF)
    got = [hid_to(sent[2 * n : 2 * n + 2], (MINE[0][n], MINE[1][n])) for n in range(3)]
    got.append(hid_to(sent[6], (BOTH, BOTH)))
    got = together(*got, *grads(xall, 0, tok, ct, nf, begun))
    grad_gate, grad_up, grad_down = got[4:]
    total = sum(g.astype(F32) for g in got[:3])
    total_own, total_other = by_core(total[0], total[1])
    total = total_own + got[3].astype(F32) + keep[7] + swap_core(total_other)
    output, grad_tokens = total[:, :nd].astype(BF), total[:, nd:].astype(BF)
    return (output, grad_tokens, grad_gate, grad_up, grad_down)


def solution(mesh):
    return jax.shard_map(
        per_device,
        mesh=mesh,
        in_specs=(
            P("hid", "wid"),
            P("wid", "hid"),
            P("wid", "hid"),
            P("hid", "wid"),
            P("hid", "wid"),
        ),
        out_specs=(
            P("hid", "wid"),
            P("hid", "wid"),
            P("wid", "hid"),
            P("wid", "hid"),
            P("hid", "wid"),
        ),
        check_vma=False,
    )
```

```python
import functools

import jax
import jax.numpy as jnp
import numpy as np
from jax import lax
from jax.experimental import pallas as pl
from jax.experimental.pallas import tpu as pltpu
from jax.sharding import PartitionSpec as P

BF, F16, F32 = jnp.bfloat16, jnp.float16, jnp.float32
NY, NX, NZ = 4, 2, 8
SPLIT = 896
MINE, BOTH = ((6, 4, 3), (1, 5, 7)), 2
VMEM = pl.BlockSpec(memory_space=pltpu.VMEM)
SMEM = pl.BlockSpec(memory_space=pltpu.SMEM)
LIMIT = pltpu.CompilerParams(vmem_limit_bytes=50 * 2**20)
SMALL = pltpu.CompilerParams(vmem_limit_bytes=12 * 2**20)
SCALE = 2.0**20


def hid_from(x, shift):
    pairs = []
    for y in range(NY):
        for h in range(NX):
            for c in range(2):
                dy, dx = divmod(shift[c], 2)
                pairs.append((((y + dy) % NY) * 4 + (h ^ dx) * 2 + c, y * 4 + h * 2 + c))
    return lax.ppermute(x, "hid", pairs)


def hid_to(x, shift):
    pairs = []
    for y in range(NY):
        for h in range(NX):
            for c in range(2):
                dy, dx = divmod(shift[c], 2)
                pairs.append((y * 4 + h * 2 + c, ((y + dy) % NY) * 4 + (h ^ dx) * 2 + c))
    return lax.ppermute(x, "hid", pairs)


def swap_core(x):
    return lax.ppermute(x, "hid", [(i, i ^ 1) for i in range(NY * NX * 2)])


def send_z(x, dz):
    pairs = [(z * 2 + l, ((z + dz) % NZ) * 2 + l) for z in range(NZ) for l in range(2)]
    return lax.ppermute(x, "wid", pairs)


def swap_x(x):
    return lax.ppermute(x, "wid", [(w, w ^ 1) for w in range(NZ * 2)])


def encode(v):
    root = jnp.sqrt(jnp.abs(v))
    return jnp.where(v < 0, -root, root).astype(F16)


def decode(w):
    w = w.astype(F32)
    return w * jnp.abs(w)


def together(*arrays):
    return lax.optimization_barrier(arrays)


def reduce_z(rings):
    made, state = [None] * len(rings), [None] * len(rings)
    turn = None
    for k in (4, 3, 2, 1):
        for n, (terms, far) in enumerate(rings):
            if k == 4:
                made[n] = terms(turn)
            term = made[n]
            out = [term(k * far)]
            if k > 1:
                out.append(term((1 - k) * far))
            if k < 4:
                out = [o + decode(s) for o, s in zip(out, state[n])]
            out = [encode(o) for o in out]
            ahead = [] if turn is None else [turn]
            out = list(together(*out, *ahead))[: len(out)]
            turn = out[0]
            got = [send_z(o, d) for o, d in zip(out, (far, -far))]
            state[n] = got if k > 1 else got + state[n][1:]
    return [term(0) + decode(s[0]) + decode(s[1]) for term, s in zip(made, state)], (turn, state[-1][1])


class Gather:
    def __init__(self, own):
        self.up = self.down = own
        self.got = {0: own}

    def round(self, k, *after):
        up, down = self.up, self.down
        if k == 4:
            half = up.shape[1] // 2
            up, down = up[:, :half], down[:, half:]
        if k == 1:
            up, *_ = together(up, *after)
            down = up
        else:
            up, down, *_ = together(up, down, *after)
        self.up, self.down = send_z(up, 1), send_z(down, -1)
        if k < 4:
            self.got[8 - k], self.got[k] = self.up, self.down
        return up

    def blocks(self):
        return [*(self.got[k] for k in range(4)), self.up, self.down, *(self.got[k] for k in range(5, 8))]


def pointwise(gate, up, dhidden):
    sig = jax.nn.sigmoid(gate)
    act = gate * sig
    hidden = (act * up).astype(BF)
    dgate = (dhidden * up * sig * (1.0 + gate * (1.0 - sig))).astype(BF)
    dup = (dhidden * act).astype(BF)
    return jnp.stack([hidden, dgate, dup])


def place():
    wid, hid = lax.axis_index("wid"), lax.axis_index("hid")
    return wid // 2, wid % 2, hid % 2


def pick(c, n, own):
    a, b = MINE[0][n], MINE[1][n]
    return jnp.where((c == 0) == own, a, b)


def order_kernel(at, pair, mine, theirs, tok, ct, tok_rel, ct_rel, flat):
    z, l, c = at[0], at[1], at[2]
    nt = pair.shape[2]
    flat[0:2] = pair[...]
    flat[2:9] = mine[...]
    flat[9:16] = theirs[...]

    def source(q, d):
        s = jnp.where(q == 0, d, jnp.where(d == c, 8, 15))
        for core in range(2):
            for n in range(3):
                s = jnp.where(q == MINE[core][n], jnp.where(c == core, 2, 9) + 2 * n + d, s)
        return s

    for k in range(8):
        for i in range(2):
            block = flat[source(lax.rem(z + k, 8), lax.rem(l + i, 2))]
            for to, tc, row in ((tok, ct, 2 * k + i), (tok_rel, ct_rel, 8 * i + k)):
                rows = pl.ds(row * nt, nt)
                to[rows, :] = block[0]
                tc[rows, :] = block[1]


def order(at, pair, mine, theirs):
    nt, nd = pair.shape[2:]
    return pl.pallas_call(
        order_kernel,
        in_specs=[SMEM, VMEM, VMEM, VMEM],
        out_specs=[VMEM] * 4,
        out_shape=[jax.ShapeDtypeStruct((16 * nt, nd), BF)] * 4,
        scratch_shapes=[pltpu.VMEM((16, 2, nt, nd), BF)],
        compiler_params=SMALL,
        name="order",
    )(at, pair, mine, theirs)


def pair_kernel(at, own, other, pair):
    c = at[2]
    pair[c] = own[...]
    pair[1 - c] = other[...]


def pair_up(at, own, other):
    return pl.pallas_call(
        pair_kernel,
        in_specs=[SMEM, VMEM, VMEM],
        out_specs=VMEM,
        out_shape=jax.ShapeDtypeStruct((2, *own.shape), own.dtype),
        compiler_params=SMALL,
        name="pair",
    )(at, own, other)


def dot(a, b, ca, cb):
    return lax.dot_general(a, b, (((ca,), (cb,)), ((), ())), preferred_element_type=F32)


def products_kernel(first, cols, t, g, dw, gw, uw, p, gv, uv, dv, sems):
    cut = pl.ds(first, cols)
    copies = [
        pltpu.make_async_copy(w, v, sems.at[i])
        for i, (w, v) in enumerate(((gw.at[:, cut], gv), (uw.at[:, cut], uv), (dw.at[cut], dv)))
    ]
    for copy in copies:
        copy.start()
    for i, copy in enumerate(copies):
        copy.wait()
        if i < 2:
            b = jnp.dot(t[...], (gv, uv)[i][...], preferred_element_type=F32)
        else:
            b = lax.dot_general(g[...], dv[...], (((1,), (1,)), ((), ())), preferred_element_type=F32)
        p[i] = (b * SCALE).reshape(p.shape[1:])


def products(t, g, first, cols, weights, nt):
    nd = t.shape[1]
    return pl.pallas_call(
        functools.partial(products_kernel, first, cols),
        in_specs=[VMEM, VMEM] + [pl.BlockSpec(memory_space=pltpu.HBM)] * 3,
        out_specs=VMEM,
        out_shape=jax.ShapeDtypeStruct((3, 2, 8, nt, cols), F32),
        scratch_shapes=[pltpu.VMEM((nd, cols), BF)] * 2 + [pltpu.VMEM((cols, nd), BF), pltpu.SemaphoreType.DMA((3,))],
        compiler_params=SMALL,
        cost_estimate=cost(16 * nt, nd, cols),
        name="products",
    )(t, g, *weights)


def spec_of(a):
    return pl.BlockSpec(a.shape, lambda j: (0,) * len(a.shape))


def side_of(nd, first, cols):
    return pl.BlockSpec((pl.Element(nd), pl.Element(cols)), lambda j: (0, first))


def end_of(nd, first, cols):
    return pl.BlockSpec((pl.Element(cols), pl.Element(nd)), lambda j: (first, 0))


def load(refs, i):
    return jnp.concatenate([r[i] for r in refs], 0)


def add_products(j, acc, ins, dw, gw, uw):
    nd = dw.shape[1]

    @pl.when(j == 0)
    def _():
        acc[...] = jnp.zeros_like(acc)

    h, g, u = (load(ins, i) for i in range(3))
    last = (((1,), (1,)), ((), ()))
    acc[:, 0:nd] += jnp.dot(h, dw[...], preferred_element_type=F32)
    gt = lax.dot_general(g, gw[...], last, preferred_element_type=F32)
    acc[:, nd:] += gt + lax.dot_general(u, uw[...], last, preferred_element_type=F32)


def add_grads(tok, ct, ins, gg, gu, gd, tt):
    @pl.when(pl.program_id(0) == 0)
    def _():
        tt[...] = tok[...].T

    h, g, u = (load(ins, i) for i in range(3))
    gg[...] = jnp.dot(tt[...], g, preferred_element_type=F32).astype(BF)
    gu[...] = jnp.dot(tt[...], u, preferred_element_type=F32).astype(BF)
    gd[...] = jnp.dot(h.T, ct[...], preferred_element_type=F32).astype(BF)


def grad_outs(nd, nf, first, cols):
    side = side_of(nd, first, cols)
    wide, tall = jax.ShapeDtypeStruct((nd, nf), BF), jax.ShapeDtypeStruct((nf, nd), BF)
    return [side, side, end_of(nd, first, cols)], [wide, wide, tall]


def weight_specs(nd, first, cols):
    side = side_of(nd, first, cols)
    return [end_of(nd, first, cols), side, side]


def cost(rows, nd, cols):
    return pl.CostEstimate(flops=6 * rows * nd * cols, bytes_accessed=12 * nd * cols, transcendentals=0)


def part_kernel(tok, ct, *refs):
    ins, (dw, gw, uw, acc, gg, gu, gd, tt) = refs[:-8], refs[-8:]
    add_products(pl.program_id(0), acc, ins, dw, gw, uw)
    add_grads(tok, ct, ins, gg, gu, gd, tt)


def part(tok, ct, arrays, first, weights):
    (rows, nd), cols = tok.shape, arrays[0].shape[-1]
    specs, shapes = grad_outs(nd, weights[0].shape[0], first, cols)
    return pl.pallas_call(
        part_kernel,
        grid=(1,),
        in_specs=[VMEM, VMEM] + [spec_of(a) for a in arrays] + weight_specs(nd, first, cols),
        out_specs=[pl.BlockSpec((rows, 2 * nd), lambda j: (0, 0)), *specs],
        out_shape=[jax.ShapeDtypeStruct((rows, 2 * nd), F32), *shapes],
        scratch_shapes=[pltpu.VMEM((nd, rows), BF)],
        compiler_params=LIMIT,
        cost_estimate=cost(rows, nd, 2 * cols),
        name="part",
    )(tok, ct, *arrays, *weights)


def out_kernel(steps, nt, at, fixed, *refs):
    j = pl.program_id(0)
    ins, (dw, gw, uw, give, keep, acc) = refs[:-6], refs[-6:]
    add_products(j, acc, ins, dw, gw, uw)

    @pl.when(j == steps - 1)
    def _():
        z, l, c = at[0], at[1], at[2]

        def block(q, d):
            rows = pl.ds(pl.multiple_of((2 * lax.rem(q + 8 - z, 8) + lax.rem(d + l, 2)) * nt, nt), nt)
            return fixed[rows, :] + acc[rows, :]

        for ref, own in ((give, False), (keep, True)):
            core = c if own else 1 - c
            for n in range(3):
                for d in range(2):
                    ref[2 * n + d] = block(pick(c, n, own), d).astype(ref.dtype)
            ref[6] = block(BOTH, core).astype(ref.dtype)
            ref[7] = block(0, core).astype(ref.dtype)


def outputs(at, fixed, arrays, first, weights, nt):
    nd, cols = weights[0].shape[1], arrays[0].shape[-1]
    whole = pl.BlockSpec((8, nt, 2 * nd), lambda j: (0, 0, 0))
    return pl.pallas_call(
        functools.partial(out_kernel, 1, nt),
        grid=(1,),
        in_specs=[SMEM, VMEM] + [spec_of(a) for a in arrays] + weight_specs(nd, first, cols),
        out_specs=[whole, whole],
        out_shape=[jax.ShapeDtypeStruct((8, nt, 2 * nd), BF), jax.ShapeDtypeStruct((8, nt, 2 * nd), F32)],
        scratch_shapes=[pltpu.VMEM((16 * nt, 2 * nd), F32)],
        compiler_params=LIMIT,
        cost_estimate=cost(16 * nt, nd, cols),
        name="outputs",
    )(at, fixed, *arrays, *weights)


def grads_kernel(count, tok, ct, *refs):
    add_grads(tok, ct, refs[:count], *refs[-4:])


def grads(arrays, first, tok, ct, nf, into):
    (rows, nd), cols = tok.shape, arrays[0].shape[-1]
    specs, shapes = grad_outs(nd, nf, first, cols)
    before = 2 + len(arrays)
    return pl.pallas_call(
        functools.partial(grads_kernel, len(arrays)),
        grid=(1,),
        in_specs=[VMEM, VMEM] + [spec_of(a) for a in arrays] + [pl.BlockSpec(memory_space=pl.ANY)] * len(into),
        out_specs=specs,
        out_shape=shapes,
        scratch_shapes=[pltpu.VMEM((nd, rows), BF)],
        input_output_aliases={before + i: i for i in range(len(into))},
        compiler_params=LIMIT,
        cost_estimate=cost(rows, nd, cols),
        name="grads",
    )(tok, ct, *arrays, *into)


def per_device(tokens, gate_weight, up_weight, down_weight, cotangent):
    nt, nd = tokens.shape
    nf = gate_weight.shape[1]
    z, l, c = place()
    at = jnp.stack([z, l, c])

    def by_core(a, b):
        return jnp.where(c == 0, a, b), jnp.where(c == 0, b, a)

    own = jnp.stack([tokens, cotangent])
    far = hid_from(own, (BOTH, BOTH))
    pair = pair_up(at, own, swap_core(own))
    got = [hid_from(pair, (a, b)) for a, b in zip(*MINE)]
    mine = jnp.concatenate(got + [far[None]], 0)
    zw = gate_weight[:, SPLIT:], up_weight[:, SPLIT:], down_weight[SPLIT:]
    mine, zw = together(mine, zw)
    tok, ct, tok_rel, ct_rel = order(at, pair, mine, swap_core(mine))

    weights = down_weight, gate_weight, up_weight

    def zterms(_):
        out = [dot(tok_rel, zw[0], 1, 0), dot(tok_rel, zw[1], 1, 0), dot(ct_rel, zw[2], 1, 1)]
        out = [(p * SCALE).reshape(2, 8, nt, nf - SPLIT) for p in out]
        return lambda k: jnp.stack([p[:, k % 8] for p in out])

    def xterms(after):
        t, g, _ = together(tok_rel, ct_rel, after)
        p = products(t, g, 0, SPLIT, weights, nt)
        return lambda k: p[:, :, k % 8]

    def finish(total, *after):
        mine, *_ = together(encode(total), *after)
        total = total + decode(swap_x(mine))[:, ::-1]
        return pointwise(*(total * (1.0 / SCALE))).reshape(3, 2 * nt, -1), mine

    (zsum, xsum), after = reduce_z([(zterms, 1), (xterms, -1)])
    zown, _ = finish(zsum)
    zring = Gather(zown)
    sent = zring.round(1, *after)
    xown, mine = finish(xsum, sent)
    sent = zring.round(2, mine)
    xring = Gather(xown)
    sent = xring.round(1, sent)
    sent = zring.round(3, sent)
    sent = xring.round(2, sent)
    sent = zring.round(4, sent)
    sent = xring.round(3, sent)
    *zall, _ = together(*zring.blocks(), sent)
    fixed, *begun = part(tok, ct, zall, SPLIT, weights)
    xring.round(4, fixed)
    xall = xring.blocks()

    give, keep = outputs(at, fixed, xall, 0, weights, nt)

    keep = keep + swap_core(give).astype(F32)
    sent = keep.astype(BF)
    got = [hid_to(sent[2 * n : 2 * n + 2], (MINE[0][n], MINE[1][n])) for n in range(3)]
    got.append(hid_to(sent[6], (BOTH, BOTH)))
    got = together(*got, *grads(xall, 0, tok, ct, nf, begun))
    grad_gate, grad_up, grad_down = got[4:]
    total = sum(g.astype(F32) for g in got[:3])
    total_own, total_other = by_core(total[0], total[1])
    total = total_own + got[3].astype(F32) + keep[7] + swap_core(total_other)
    output, grad_tokens = total[:, :nd].astype(BF), total[:, nd:].astype(BF)
    return (output, grad_tokens, grad_gate, grad_up, grad_down)


def solution(mesh):
    return jax.shard_map(
        per_device,
        mesh=mesh,
        in_specs=(
            P("hid", "wid"),
            P("wid", "hid"),
            P("wid", "hid"),
            P("hid", "wid"),
            P("hid", "wid"),
        ),
        out_specs=(
            P("hid", "wid"),
            P("hid", "wid"),
            P("wid", "hid"),
            P("wid", "hid"),
            P("hid", "wid"),
        ),
        check_vma=False,
    )
```

```python
import functools

import jax
import jax.numpy as jnp
import numpy as np
from jax import lax
from jax.experimental import pallas as pl
from jax.experimental.pallas import tpu as pltpu
from jax.sharding import PartitionSpec as P

BF, F16, F32 = jnp.bfloat16, jnp.float16, jnp.float32
NY, NX, NZ = 4, 2, 8
SPLIT = 896
MINE, BOTH = ((6, 4, 3), (1, 5, 7)), 2
VMEM = pl.BlockSpec(memory_space=pltpu.VMEM)
SMEM = pl.BlockSpec(memory_space=pltpu.SMEM)
LIMIT = pltpu.CompilerParams(vmem_limit_bytes=50 * 2**20)
SMALL = pltpu.CompilerParams(vmem_limit_bytes=12 * 2**20)
SCALE = 2.0**20


def hid_from(x, shift):
    pairs = []
    for y in range(NY):
        for h in range(NX):
            for c in range(2):
                dy, dx = divmod(shift[c], 2)
                pairs.append((((y + dy) % NY) * 4 + (h ^ dx) * 2 + c, y * 4 + h * 2 + c))
    return lax.ppermute(x, "hid", pairs)


def hid_to(x, shift):
    pairs = []
    for y in range(NY):
        for h in range(NX):
            for c in range(2):
                dy, dx = divmod(shift[c], 2)
                pairs.append((y * 4 + h * 2 + c, ((y + dy) % NY) * 4 + (h ^ dx) * 2 + c))
    return lax.ppermute(x, "hid", pairs)


def swap_core(x):
    return lax.ppermute(x, "hid", [(i, i ^ 1) for i in range(NY * NX * 2)])


def send_z(x, dz):
    pairs = [(z * 2 + l, ((z + dz) % NZ) * 2 + l) for z in range(NZ) for l in range(2)]
    return lax.ppermute(x, "wid", pairs)


def swap_x(x):
    return lax.ppermute(x, "wid", [(w, w ^ 1) for w in range(NZ * 2)])


def encode(v):
    root = jnp.sqrt(jnp.abs(v))
    return jnp.where(v < 0, -root, root).astype(F16)


def decode(w):
    w = w.astype(F32)
    return w * jnp.abs(w)


def together(*arrays):
    return lax.optimization_barrier(arrays)


def reduce_z(rings):
    made, state = [None] * len(rings), [None] * len(rings)
    turn = None
    for k in (4, 3, 2, 1):
        for n, terms in enumerate(rings):
            if k == 4:
                made[n] = terms(turn)
            term = made[n]
            if k == 4:
                out = [term(4)[:, :1], term(4)[:, 1:]]
            else:
                up, down = (decode(s) for s in state[n])
                if k == 3:
                    none = (0, 0, 0)
                    up = lax.pad(up, 0.0, (none, (0, 1, 0), none, none))
                    down = lax.pad(down, 0.0, (none, (1, 0, 0), none, none))
                out = [term(k) + up, term(-k) + down]
            out = [encode(o) for o in out]
            out = list(together(*out, *([] if turn is None else [turn])))[:2]
            turn = out[0]
            state[n] = send_z(out[0], 1), send_z(out[1], -1)
    return [term(0) + decode(s[0]) + decode(s[1]) for term, s in zip(made, state)], state[-1][0]


class Gather:
    def __init__(self, own):
        self.up = self.down = own
        self.got = {0: own}

    def round(self, k, *after):
        up, down = self.up, self.down
        if k == 4:
            half = up.shape[1] // 2
            up, down = up[:, :half], down[:, half:]
        if k == 1:
            up, *_ = together(up, *after)
            down = up
        else:
            up, down, *_ = together(up, down, *after)
        self.up, self.down = send_z(up, 1), send_z(down, -1)
        if k < 4:
            self.got[8 - k], self.got[k] = self.up, self.down
        return up

    def blocks(self):
        return [*(self.got[k] for k in range(4)), self.up, self.down, *(self.got[k] for k in range(5, 8))]


def pointwise(gate, up, dhidden):
    sig = jax.nn.sigmoid(gate)
    act = gate * sig
    hidden = (act * up).astype(BF)
    dgate = (dhidden * up * sig * (1.0 + gate * (1.0 - sig))).astype(BF)
    dup = (dhidden * act).astype(BF)
    return jnp.stack([hidden, dgate, dup])


def place():
    wid, hid = lax.axis_index("wid"), lax.axis_index("hid")
    return wid // 2, wid % 2, hid % 2


def pick(c, n, own):
    a, b = MINE[0][n], MINE[1][n]
    return jnp.where((c == 0) == own, a, b)


def order_kernel(at, pair, mine, theirs, tok, ct, tok_rel, ct_rel, flat):
    z, l, c = at[0], at[1], at[2]
    nt = pair.shape[2]
    flat[0:2] = pair[...]
    flat[2:9] = mine[...]
    flat[9:16] = theirs[...]

    def source(q, d):
        s = jnp.where(q == 0, d, jnp.where(d == c, 8, 15))
        for core in range(2):
            for n in range(3):
                s = jnp.where(q == MINE[core][n], jnp.where(c == core, 2, 9) + 2 * n + d, s)
        return s

    for k in range(8):
        for i in range(2):
            block = flat[source(lax.rem(z + k, 8), lax.rem(l + i, 2))]
            for to, tc, row in ((tok, ct, 2 * k + i), (tok_rel, ct_rel, 8 * i + k)):
                rows = pl.ds(row * nt, nt)
                to[rows, :] = block[0]
                tc[rows, :] = block[1]


def order(at, pair, mine, theirs):
    nt, nd = pair.shape[2:]
    return pl.pallas_call(
        order_kernel,
        in_specs=[SMEM, VMEM, VMEM, VMEM],
        out_specs=[VMEM] * 4,
        out_shape=[jax.ShapeDtypeStruct((16 * nt, nd), BF)] * 4,
        scratch_shapes=[pltpu.VMEM((16, 2, nt, nd), BF)],
        compiler_params=SMALL,
        name="order",
    )(at, pair, mine, theirs)


def pair_kernel(at, own, other, pair):
    c = at[2]
    pair[c] = own[...]
    pair[1 - c] = other[...]


def pair_up(at, own, other):
    return pl.pallas_call(
        pair_kernel,
        in_specs=[SMEM, VMEM, VMEM],
        out_specs=VMEM,
        out_shape=jax.ShapeDtypeStruct((2, *own.shape), own.dtype),
        compiler_params=SMALL,
        name="pair",
    )(at, own, other)


def dot(a, b, ca, cb):
    return lax.dot_general(a, b, (((ca,), (cb,)), ((), ())), preferred_element_type=F32)


def products_kernel(first, cols, t, g, dw, gw, uw, p, gv, uv, dv, sems):
    cut = pl.ds(first, cols)
    copies = [
        pltpu.make_async_copy(w, v, sems.at[i])
        for i, (w, v) in enumerate(((gw.at[:, cut], gv), (uw.at[:, cut], uv), (dw.at[cut], dv)))
    ]
    for copy in copies:
        copy.start()
    for i, copy in enumerate(copies):
        copy.wait()
        if i < 2:
            b = jnp.dot(t[...], (gv, uv)[i][...], preferred_element_type=F32)
        else:
            b = lax.dot_general(g[...], dv[...], (((1,), (1,)), ((), ())), preferred_element_type=F32)
        p[i] = (b * SCALE).reshape(p.shape[1:])


def products(t, g, first, cols, weights, nt):
    nd = t.shape[1]
    return pl.pallas_call(
        functools.partial(products_kernel, first, cols),
        in_specs=[VMEM, VMEM] + [pl.BlockSpec(memory_space=pltpu.HBM)] * 3,
        out_specs=VMEM,
        out_shape=jax.ShapeDtypeStruct((3, 2, 8, nt, cols), F32),
        scratch_shapes=[pltpu.VMEM((nd, cols), BF)] * 2 + [pltpu.VMEM((cols, nd), BF), pltpu.SemaphoreType.DMA((3,))],
        compiler_params=SMALL,
        cost_estimate=cost(16 * nt, nd, cols),
        name="products",
    )(t, g, *weights)


def spec_of(a):
    return pl.BlockSpec(a.shape, lambda j: (0,) * len(a.shape))


def side_of(nd, first, cols):
    return pl.BlockSpec((pl.Element(nd), pl.Element(cols)), lambda j: (0, first))


def end_of(nd, first, cols):
    return pl.BlockSpec((pl.Element(cols), pl.Element(nd)), lambda j: (first, 0))


def load(refs, i):
    return jnp.concatenate([r[i] for r in refs], 0)


def add_products(j, acc, ins, dw, gw, uw):
    nd = dw.shape[1]

    @pl.when(j == 0)
    def _():
        acc[...] = jnp.zeros_like(acc)

    h, g, u = (load(ins, i) for i in range(3))
    last = (((1,), (1,)), ((), ()))
    acc[:, 0:nd] += jnp.dot(h, dw[...], preferred_element_type=F32)
    gt = lax.dot_general(g, gw[...], last, preferred_element_type=F32)
    acc[:, nd:] += gt + lax.dot_general(u, uw[...], last, preferred_element_type=F32)


def add_grads(tok, ct, ins, gg, gu, gd, tt):
    @pl.when(pl.program_id(0) == 0)
    def _():
        tt[...] = tok[...].T

    h, g, u = (load(ins, i) for i in range(3))
    gg[...] = jnp.dot(tt[...], g, preferred_element_type=F32).astype(BF)
    gu[...] = jnp.dot(tt[...], u, preferred_element_type=F32).astype(BF)
    gd[...] = jnp.dot(h.T, ct[...], preferred_element_type=F32).astype(BF)


def grad_outs(nd, nf, first, cols):
    side = side_of(nd, first, cols)
    wide, tall = jax.ShapeDtypeStruct((nd, nf), BF), jax.ShapeDtypeStruct((nf, nd), BF)
    return [side, side, end_of(nd, first, cols)], [wide, wide, tall]


def weight_specs(nd, first, cols):
    side = side_of(nd, first, cols)
    return [end_of(nd, first, cols), side, side]


def cost(rows, nd, cols):
    return pl.CostEstimate(flops=6 * rows * nd * cols, bytes_accessed=12 * nd * cols, transcendentals=0)


def part_kernel(tok, ct, *refs):
    ins, (dw, gw, uw, acc, gg, gu, gd, tt) = refs[:-8], refs[-8:]
    add_products(pl.program_id(0), acc, ins, dw, gw, uw)
    add_grads(tok, ct, ins, gg, gu, gd, tt)


def part(tok, ct, arrays, first, weights):
    (rows, nd), cols = tok.shape, arrays[0].shape[-1]
    specs, shapes = grad_outs(nd, weights[0].shape[0], first, cols)
    return pl.pallas_call(
        part_kernel,
        grid=(1,),
        in_specs=[VMEM, VMEM] + [spec_of(a) for a in arrays] + weight_specs(nd, first, cols),
        out_specs=[pl.BlockSpec((rows, 2 * nd), lambda j: (0, 0)), *specs],
        out_shape=[jax.ShapeDtypeStruct((rows, 2 * nd), F32), *shapes],
        scratch_shapes=[pltpu.VMEM((nd, rows), BF)],
        compiler_params=LIMIT,
        cost_estimate=cost(rows, nd, 2 * cols),
        name="part",
    )(tok, ct, *arrays, *weights)


def out_kernel(steps, nt, at, fixed, *refs):
    j = pl.program_id(0)
    ins, (dw, gw, uw, give, keep, acc) = refs[:-6], refs[-6:]
    add_products(j, acc, ins, dw, gw, uw)

    @pl.when(j == steps - 1)
    def _():
        z, l, c = at[0], at[1], at[2]

        def block(q, d):
            rows = pl.ds(pl.multiple_of((2 * lax.rem(q + 8 - z, 8) + lax.rem(d + l, 2)) * nt, nt), nt)
            return fixed[rows, :] + acc[rows, :]

        for ref, own in ((give, False), (keep, True)):
            core = c if own else 1 - c
            for n in range(3):
                for d in range(2):
                    ref[2 * n + d] = block(pick(c, n, own), d).astype(ref.dtype)
            ref[6] = block(BOTH, core).astype(ref.dtype)
            ref[7] = block(0, core).astype(ref.dtype)


def outputs(at, fixed, arrays, first, weights, nt):
    nd, cols = weights[0].shape[1], arrays[0].shape[-1]
    whole = pl.BlockSpec((8, nt, 2 * nd), lambda j: (0, 0, 0))
    return pl.pallas_call(
        functools.partial(out_kernel, 1, nt),
        grid=(1,),
        in_specs=[SMEM, VMEM] + [spec_of(a) for a in arrays] + weight_specs(nd, first, cols),
        out_specs=[whole, whole],
        out_shape=[jax.ShapeDtypeStruct((8, nt, 2 * nd), BF), jax.ShapeDtypeStruct((8, nt, 2 * nd), F32)],
        scratch_shapes=[pltpu.VMEM((16 * nt, 2 * nd), F32)],
        compiler_params=LIMIT,
        cost_estimate=cost(16 * nt, nd, cols),
        name="outputs",
    )(at, fixed, *arrays, *weights)


def grads_kernel(count, tok, ct, *refs):
    add_grads(tok, ct, refs[:count], *refs[-4:])


def grads(arrays, first, tok, ct, nf, into):
    (rows, nd), cols = tok.shape, arrays[0].shape[-1]
    specs, shapes = grad_outs(nd, nf, first, cols)
    before = 2 + len(arrays)
    return pl.pallas_call(
        functools.partial(grads_kernel, len(arrays)),
        grid=(1,),
        in_specs=[VMEM, VMEM] + [spec_of(a) for a in arrays] + [pl.BlockSpec(memory_space=pl.ANY)] * len(into),
        out_specs=specs,
        out_shape=shapes,
        scratch_shapes=[pltpu.VMEM((nd, rows), BF)],
        input_output_aliases={before + i: i for i in range(len(into))},
        compiler_params=LIMIT,
        cost_estimate=cost(rows, nd, cols),
        name="grads",
    )(tok, ct, *arrays, *into)


def per_device(tokens, gate_weight, up_weight, down_weight, cotangent):
    nt, nd = tokens.shape
    nf = gate_weight.shape[1]
    z, l, c = place()
    at = jnp.stack([z, l, c])

    def by_core(a, b):
        return jnp.where(c == 0, a, b), jnp.where(c == 0, b, a)

    own = jnp.stack([tokens, cotangent])
    far = hid_from(own, (BOTH, BOTH))
    pair = pair_up(at, own, swap_core(own))
    got = [hid_from(pair, (a, b)) for a, b in zip(*MINE)]
    mine = jnp.concatenate(got + [far[None]], 0)
    zw = gate_weight[:, SPLIT:], up_weight[:, SPLIT:], down_weight[SPLIT:]
    mine, zw = together(mine, zw)
    tok, ct, tok_rel, ct_rel = order(at, pair, mine, swap_core(mine))

    weights = down_weight, gate_weight, up_weight

    def zterms(_):
        out = [dot(tok_rel, zw[0], 1, 0), dot(tok_rel, zw[1], 1, 0), dot(ct_rel, zw[2], 1, 1)]
        out = [(p * SCALE).reshape(2, 8, nt, nf - SPLIT) for p in out]
        return lambda k: jnp.stack([p[:, k % 8] for p in out])

    def xterms(after):
        t, g, _ = together(tok_rel, ct_rel, after)
        p = products(t, g, 0, SPLIT, weights, nt)
        return lambda k: p[:, :, k % 8]

    def finish(total, *after):
        mine, *_ = together(encode(total), *after)
        total = total + decode(swap_x(mine))[:, ::-1]
        return pointwise(*(total * (1.0 / SCALE))).reshape(3, 2 * nt, -1), mine

    (zsum, xsum), after = reduce_z([zterms, xterms])
    zown, _ = finish(zsum)
    zring = Gather(zown)
    sent = zring.round(1, after)
    xown, mine = finish(xsum)
    zring.round(2, mine)
    xring = Gather(xown)
    sent = xring.round(1)
    sent = zring.round(3, sent)
    sent = xring.round(2, sent)
    sent = zring.round(4, sent)
    sent = xring.round(3, sent)
    *zall, _ = together(*zring.blocks(), sent)
    fixed, *begun = part(tok, ct, zall, SPLIT, weights)
    xring.round(4, fixed)
    xall = xring.blocks()

    give, keep = outputs(at, fixed, xall, 0, weights, nt)

    keep = keep + swap_core(give).astype(F32)
    sent = keep.astype(BF)
    got = [hid_to(sent[2 * n : 2 * n + 2], (MINE[0][n], MINE[1][n])) for n in range(3)]
    got.append(hid_to(sent[6], (BOTH, BOTH)))
    got = together(*got, *grads(xall, 0, tok, ct, nf, begun))
    grad_gate, grad_up, grad_down = got[4:]
    total = sum(g.astype(F32) for g in got[:3])
    total_own, total_other = by_core(total[0], total[1])
    total = total_own + got[3].astype(F32) + keep[7] + swap_core(total_other)
    output, grad_tokens = total[:, :nd].astype(BF), total[:, nd:].astype(BF)
    return (output, grad_tokens, grad_gate, grad_up, grad_down)


def solution(mesh):
    return jax.shard_map(
        per_device,
        mesh=mesh,
        in_specs=(
            P("hid", "wid"),
            P("wid", "hid"),
            P("wid", "hid"),
            P("hid", "wid"),
            P("hid", "wid"),
        ),
        out_specs=(
            P("hid", "wid"),
            P("hid", "wid"),
            P("wid", "hid"),
            P("wid", "hid"),
            P("hid", "wid"),
        ),
        check_vma=False,
    )
```

```python
import functools

import jax
import jax.numpy as jnp
import numpy as np
from jax import lax
from jax.experimental import pallas as pl
from jax.experimental.pallas import tpu as pltpu
from jax.sharding import PartitionSpec as P

BF, F16, F32 = jnp.bfloat16, jnp.float16, jnp.float32
NY, NX, NZ = 4, 2, 8
SPLIT = 896
MINE, BOTH = ((6, 4, 3), (1, 5, 7)), 2
VMEM = pl.BlockSpec(memory_space=pltpu.VMEM)
SMEM = pl.BlockSpec(memory_space=pltpu.SMEM)
LIMIT = pltpu.CompilerParams(vmem_limit_bytes=50 * 2**20)
SMALL = pltpu.CompilerParams(vmem_limit_bytes=12 * 2**20)
SCALE = 2.0**20


def hid_from(x, shift):
    pairs = []
    for y in range(NY):
        for h in range(NX):
            for c in range(2):
                dy, dx = divmod(shift[c], 2)
                pairs.append((((y + dy) % NY) * 4 + (h ^ dx) * 2 + c, y * 4 + h * 2 + c))
    return lax.ppermute(x, "hid", pairs)


def hid_to(x, shift):
    pairs = []
    for y in range(NY):
        for h in range(NX):
            for c in range(2):
                dy, dx = divmod(shift[c], 2)
                pairs.append((y * 4 + h * 2 + c, ((y + dy) % NY) * 4 + (h ^ dx) * 2 + c))
    return lax.ppermute(x, "hid", pairs)


def swap_core(x):
    return lax.ppermute(x, "hid", [(i, i ^ 1) for i in range(NY * NX * 2)])


def send_z(x, dz):
    pairs = [(z * 2 + l, ((z + dz) % NZ) * 2 + l) for z in range(NZ) for l in range(2)]
    return lax.ppermute(x, "wid", pairs)


def swap_x(x):
    return lax.ppermute(x, "wid", [(w, w ^ 1) for w in range(NZ * 2)])


def encode(v):
    root = jnp.sqrt(jnp.abs(v))
    return jnp.where(v < 0, -root, root).astype(F16)


def decode(w):
    w = w.astype(F32)
    return w * jnp.abs(w)


def together(*arrays):
    return lax.optimization_barrier(arrays)


def reduce_z(rings):
    made, state = [None] * len(rings), [None] * len(rings)
    turn = None
    for k in (4, 3, 2, 1):
        for n, terms in enumerate(rings):
            if k == 4:
                made[n] = terms(turn)
            term = made[n]
            if k == 4:
                out = [term(4)[:, :1], term(4)[:, 1:]]
            else:
                up, down = (decode(s) for s in state[n])
                if k == 3:
                    none = (0, 0, 0)
                    up = lax.pad(up, 0.0, (none, (0, 1, 0), none, none))
                    down = lax.pad(down, 0.0, (none, (1, 0, 0), none, none))
                out = [term(k) + up, term(-k) + down]
            out = [encode(o) for o in out]
            out = list(together(*out, *([] if turn is None else [turn])))[:2]
            turn = out[0]
            state[n] = send_z(out[0], 1), send_z(out[1], -1)
    return [term(0) + decode(s[0]) + decode(s[1]) for term, s in zip(made, state)], state[-1][0]


class Gather:
    def __init__(self, own):
        self.up = self.down = own
        self.got = {0: own}

    def round(self, k, *after):
        up, down = self.up, self.down
        if k == 4:
            half = up.shape[1] // 2
            up, down = up[:, :half], down[:, half:]
        if k == 1:
            up, *_ = together(up, *after)
            down = up
        else:
            up, down, *_ = together(up, down, *after)
        self.up, self.down = send_z(up, 1), send_z(down, -1)
        if k < 4:
            self.got[8 - k], self.got[k] = self.up, self.down
        return up

    def blocks(self):
        return [*(self.got[k] for k in range(4)), self.up, self.down, *(self.got[k] for k in range(5, 8))]


def pointwise(gate, up, dhidden):
    sig = jax.nn.sigmoid(gate)
    act = gate * sig
    hidden = (act * up).astype(BF)
    dgate = (dhidden * up * sig * (1.0 + gate * (1.0 - sig))).astype(BF)
    dup = (dhidden * act).astype(BF)
    return jnp.stack([hidden, dgate, dup])


def place():
    wid, hid = lax.axis_index("wid"), lax.axis_index("hid")
    return wid // 2, wid % 2, hid % 2


def pick(c, n, own):
    a, b = MINE[0][n], MINE[1][n]
    return jnp.where((c == 0) == own, a, b)


def order_kernel(at, pair, mine, theirs, tok, ct, tok_rel, ct_rel, flat):
    z, l, c = at[0], at[1], at[2]
    nt = pair.shape[2]
    flat[0:2] = pair[...]
    flat[2:9] = mine[...]
    flat[9:16] = theirs[...]

    def source(q, d):
        s = jnp.where(q == 0, d, jnp.where(d == c, 8, 15))
        for core in range(2):
            for n in range(3):
                s = jnp.where(q == MINE[core][n], jnp.where(c == core, 2, 9) + 2 * n + d, s)
        return s

    for k in range(8):
        for i in range(2):
            block = flat[source(lax.rem(z + k, 8), lax.rem(l + i, 2))]
            for to, tc, row in ((tok, ct, 2 * k + i), (tok_rel, ct_rel, 8 * i + k)):
                rows = pl.ds(row * nt, nt)
                to[rows, :] = block[0]
                tc[rows, :] = block[1]


def order(at, pair, mine, theirs):
    nt, nd = pair.shape[2:]
    return pl.pallas_call(
        order_kernel,
        in_specs=[SMEM, VMEM, VMEM, VMEM],
        out_specs=[VMEM] * 4,
        out_shape=[jax.ShapeDtypeStruct((16 * nt, nd), BF)] * 4,
        scratch_shapes=[pltpu.VMEM((16, 2, nt, nd), BF)],
        compiler_params=SMALL,
        name="order",
    )(at, pair, mine, theirs)


def pair_kernel(at, own, other, pair):
    c = at[2]
    pair[c] = own[...]
    pair[1 - c] = other[...]


def pair_up(at, own, other):
    return pl.pallas_call(
        pair_kernel,
        in_specs=[SMEM, VMEM, VMEM],
        out_specs=VMEM,
        out_shape=jax.ShapeDtypeStruct((2, *own.shape), own.dtype),
        compiler_params=SMALL,
        name="pair",
    )(at, own, other)


def dot(a, b, ca, cb):
    return lax.dot_general(a, b, (((ca,), (cb,)), ((), ())), preferred_element_type=F32)


def products_kernel(first, cols, t, g, dw, gw, uw, p, gv, uv, dv, sems):
    cut = pl.ds(first, cols)
    copies = [
        pltpu.make_async_copy(w, v, sems.at[i])
        for i, (w, v) in enumerate(((gw.at[:, cut], gv), (uw.at[:, cut], uv), (dw.at[cut], dv)))
    ]
    for copy in copies:
        copy.start()
    for i, copy in enumerate(copies):
        copy.wait()
        if i < 2:
            b = jnp.dot(t[...], (gv, uv)[i][...], preferred_element_type=F32)
        else:
            b = lax.dot_general(g[...], dv[...], (((1,), (1,)), ((), ())), preferred_element_type=F32)
        p[i] = (b * SCALE).reshape(p.shape[1:])


def products(t, g, first, cols, weights, nt):
    nd = t.shape[1]
    return pl.pallas_call(
        functools.partial(products_kernel, first, cols),
        in_specs=[VMEM, VMEM] + [pl.BlockSpec(memory_space=pltpu.HBM)] * 3,
        out_specs=VMEM,
        out_shape=jax.ShapeDtypeStruct((3, 2, 8, nt, cols), F32),
        scratch_shapes=[pltpu.VMEM((nd, cols), BF)] * 2 + [pltpu.VMEM((cols, nd), BF), pltpu.SemaphoreType.DMA((3,))],
        compiler_params=SMALL,
        cost_estimate=cost(16 * nt, nd, cols),
        name="products",
    )(t, g, *weights)


def spec_of(a):
    return pl.BlockSpec(a.shape, lambda j: (0,) * len(a.shape))


def side_of(nd, first, cols):
    return pl.BlockSpec((pl.Element(nd), pl.Element(cols)), lambda j: (0, first))


def end_of(nd, first, cols):
    return pl.BlockSpec((pl.Element(cols), pl.Element(nd)), lambda j: (first, 0))


def load(refs, i):
    return jnp.concatenate([r[i] for r in refs], 0)


def add_products(j, acc, ins, dw, gw, uw):
    nd = dw.shape[1]

    @pl.when(j == 0)
    def _():
        acc[...] = jnp.zeros_like(acc)

    h, g, u = (load(ins, i) for i in range(3))
    last = (((1,), (1,)), ((), ()))
    acc[:, 0:nd] += jnp.dot(h, dw[...], preferred_element_type=F32)
    gt = lax.dot_general(g, gw[...], last, preferred_element_type=F32)
    acc[:, nd:] += gt + lax.dot_general(u, uw[...], last, preferred_element_type=F32)


def add_grads(tok, ct, ins, gg, gu, gd, tt):
    @pl.when(pl.program_id(0) == 0)
    def _():
        tt[...] = tok[...].T

    h, g, u = (load(ins, i) for i in range(3))
    gg[...] = jnp.dot(tt[...], g, preferred_element_type=F32).astype(BF)
    gu[...] = jnp.dot(tt[...], u, preferred_element_type=F32).astype(BF)
    gd[...] = jnp.dot(h.T, ct[...], preferred_element_type=F32).astype(BF)


def grad_outs(nd, nf, first, cols):
    side = side_of(nd, first, cols)
    wide, tall = jax.ShapeDtypeStruct((nd, nf), BF), jax.ShapeDtypeStruct((nf, nd), BF)
    return [side, side, end_of(nd, first, cols)], [wide, wide, tall]


def weight_specs(nd, first, cols):
    side = side_of(nd, first, cols)
    return [end_of(nd, first, cols), side, side]


def cost(rows, nd, cols):
    return pl.CostEstimate(flops=6 * rows * nd * cols, bytes_accessed=12 * nd * cols, transcendentals=0)


def part_kernel(tok, ct, *refs):
    ins, (dw, gw, uw, acc, gg, gu, gd, tt) = refs[:-8], refs[-8:]
    add_products(pl.program_id(0), acc, ins, dw, gw, uw)
    add_grads(tok, ct, ins, gg, gu, gd, tt)


def part(tok, ct, arrays, first, weights):
    (rows, nd), cols = tok.shape, arrays[0].shape[-1]
    specs, shapes = grad_outs(nd, weights[0].shape[0], first, cols)
    return pl.pallas_call(
        part_kernel,
        grid=(1,),
        in_specs=[VMEM, VMEM] + [spec_of(a) for a in arrays] + weight_specs(nd, first, cols),
        out_specs=[pl.BlockSpec((rows, 2 * nd), lambda j: (0, 0)), *specs],
        out_shape=[jax.ShapeDtypeStruct((rows, 2 * nd), F32), *shapes],
        scratch_shapes=[pltpu.VMEM((nd, rows), BF)],
        compiler_params=LIMIT,
        cost_estimate=cost(rows, nd, 2 * cols),
        name="part",
    )(tok, ct, *arrays, *weights)


def out_kernel(steps, nt, at, fixed, *refs):
    j = pl.program_id(0)
    ins, (dw, gw, uw, give, keep, acc) = refs[:-6], refs[-6:]
    add_products(j, acc, ins, dw, gw, uw)

    @pl.when(j == steps - 1)
    def _():
        z, l, c = at[0], at[1], at[2]

        def block(q, d):
            rows = pl.ds(pl.multiple_of((2 * lax.rem(q + 8 - z, 8) + lax.rem(d + l, 2)) * nt, nt), nt)
            return fixed[rows, :] + acc[rows, :]

        for ref, own in ((give, False), (keep, True)):
            core = c if own else 1 - c
            for n in range(3):
                for d in range(2):
                    ref[2 * n + d] = block(pick(c, n, own), d).astype(ref.dtype)
            ref[6] = block(BOTH, core).astype(ref.dtype)
            ref[7] = block(0, core).astype(ref.dtype)


def outputs(at, fixed, arrays, first, weights, nt):
    nd, cols = weights[0].shape[1], arrays[0].shape[-1]
    whole = pl.BlockSpec((8, nt, 2 * nd), lambda j: (0, 0, 0))
    return pl.pallas_call(
        functools.partial(out_kernel, 1, nt),
        grid=(1,),
        in_specs=[SMEM, VMEM] + [spec_of(a) for a in arrays] + weight_specs(nd, first, cols),
        out_specs=[whole, whole],
        out_shape=[jax.ShapeDtypeStruct((8, nt, 2 * nd), BF), jax.ShapeDtypeStruct((8, nt, 2 * nd), F32)],
        scratch_shapes=[pltpu.VMEM((16 * nt, 2 * nd), F32)],
        compiler_params=pltpu.CompilerParams(vmem_limit_bytes=28 * 2**20),
        cost_estimate=cost(16 * nt, nd, cols),
        name="outputs",
    )(at, fixed, *arrays, *weights)


def grads_kernel(count, tok, ct, *refs):
    add_grads(tok, ct, refs[:count], *refs[-4:])


def grads(arrays, first, tok, ct, nf, into):
    (rows, nd), cols = tok.shape, arrays[0].shape[-1]
    specs, shapes = grad_outs(nd, nf, first, cols)
    before = 2 + len(arrays)
    return pl.pallas_call(
        functools.partial(grads_kernel, len(arrays)),
        grid=(1,),
        in_specs=[VMEM, VMEM] + [spec_of(a) for a in arrays] + [pl.BlockSpec(memory_space=pl.ANY)] * len(into),
        out_specs=specs,
        out_shape=shapes,
        scratch_shapes=[pltpu.VMEM((nd, rows), BF)],
        input_output_aliases={before + i: i for i in range(len(into))},
        compiler_params=LIMIT,
        cost_estimate=cost(rows, nd, cols),
        name="grads",
    )(tok, ct, *arrays, *into)


def per_device(tokens, gate_weight, up_weight, down_weight, cotangent):
    nt, nd = tokens.shape
    nf = gate_weight.shape[1]
    z, l, c = place()
    at = jnp.stack([z, l, c])

    def by_core(a, b):
        return jnp.where(c == 0, a, b), jnp.where(c == 0, b, a)

    own = jnp.stack([tokens, cotangent])
    far = hid_from(own, (BOTH, BOTH))
    pair = pair_up(at, own, swap_core(own))
    got = [hid_from(pair, (a, b)) for a, b in zip(*MINE)]
    mine = jnp.concatenate(got + [far[None]], 0)
    zw = gate_weight[:, SPLIT:], up_weight[:, SPLIT:], down_weight[SPLIT:]
    mine, zw = together(mine, zw)
    tok, ct, tok_rel, ct_rel = order(at, pair, mine, swap_core(mine))

    weights = down_weight, gate_weight, up_weight

    def zterms(_):
        out = [dot(tok_rel, zw[0], 1, 0), dot(tok_rel, zw[1], 1, 0), dot(ct_rel, zw[2], 1, 1)]
        out = [(p * SCALE).reshape(2, 8, nt, nf - SPLIT) for p in out]
        return lambda k: jnp.stack([p[:, k % 8] for p in out])

    def xterms(after):
        t, g, _ = together(tok_rel, ct_rel, after)
        p = products(t, g, 0, SPLIT, weights, nt)
        return lambda k: p[:, :, k % 8]

    def finish(total, *after):
        mine, *_ = together(encode(total), *after)
        total = total + decode(swap_x(mine))[:, ::-1]
        return pointwise(*(total * (1.0 / SCALE))).reshape(3, 2 * nt, -1), mine

    (zsum, xsum), after = reduce_z([zterms, xterms])
    zown, _ = finish(zsum)
    zring = Gather(zown)
    sent = zring.round(1, after)
    xown, mine = finish(xsum)
    zring.round(2, mine)
    xring = Gather(xown)
    sent = xring.round(1)
    sent = zring.round(3, sent)
    sent = xring.round(2, sent)
    sent = zring.round(4, sent)
    sent = xring.round(3, sent)
    *zall, _ = together(*zring.blocks(), sent)
    fixed, *begun = part(tok, ct, zall, SPLIT, weights)
    xring.round(4, fixed)
    xall = xring.blocks()

    give, keep = outputs(at, fixed, xall, 0, weights, nt)

    keep = keep + swap_core(give).astype(F32)
    sent = keep.astype(BF)
    got = [hid_to(sent[2 * n : 2 * n + 2], (MINE[0][n], MINE[1][n])) for n in range(3)]
    got.append(hid_to(sent[6], (BOTH, BOTH)))
    got = together(*got, *grads(xall, 0, tok, ct, nf, begun))
    grad_gate, grad_up, grad_down = got[4:]
    total = sum(g.astype(F32) for g in got[:3])
    total_own, total_other = by_core(total[0], total[1])
    total = total_own + got[3].astype(F32) + keep[7] + swap_core(total_other)
    output, grad_tokens = total[:, :nd].astype(BF), total[:, nd:].astype(BF)
    return (output, grad_tokens, grad_gate, grad_up, grad_down)


def solution(mesh):
    return jax.shard_map(
        per_device,
        mesh=mesh,
        in_specs=(
            P("hid", "wid"),
            P("wid", "hid"),
            P("wid", "hid"),
            P("hid", "wid"),
            P("hid", "wid"),
        ),
        out_specs=(
            P("hid", "wid"),
            P("hid", "wid"),
            P("wid", "hid"),
            P("wid", "hid"),
            P("hid", "wid"),
        ),
        check_vma=False,
    )
```
